32 devices in a mesh: dp: 8 (over z, x), tensor: 4 (over y, core).
Axes of the slice: x: 2, y: 2, z: 4, core: 2. Of those that a mesh axis runs over, the one named last changes fastest.
Arguments:
- layer_in: bfloat16 [8192, 768], P('dp'), may hold values from -6 to 6
- doc_ids: int32 [8192], P('dp'), may hold values from -1 to 8191, as said below
- qkv_weight: bfloat16 [3, 768, 768], P(None, None, 'tensor'), may hold values from -0.21875 to 0.21875
- out_weight: bfloat16 [768, 768], P('tensor'), may hold values from -1.25 to 1.25
- up_weight: bfloat16 [2, 768, 1152], P(None, None, 'tensor'), may hold values from -0.21875 to 0.21875
- down_weight: bfloat16 [1152, 768], P('tensor'), may hold values from -0.25 to 0.25
- norm1_gain: bfloat16 [768], replicated, may hold values from 0.5 to 1.5
- norm2_gain: bfloat16 [768], replicated, may hold values from 0.5 to 1.5
- out_cotangent: bfloat16 [8192, 768], P('dp'), may hold values from -6 to 6
Outputs:
- layer_out: bfloat16 [8192, 768], P('dp')
- input_grad: bfloat16 [8192, 768], P('dp')
- grad_qkv: float32 [3, 768, 768], P(None, None, 'tensor')
- grad_out: float32 [768, 768], P('tensor')
- grad_up: float32 [2, 768, 1152], P(None, None, 'tensor')
- grad_down: float32 [1152, 768], P('tensor')
- grad_norm1: float32 [768], replicated
- grad_norm2: float32 [768], replicated
The draws below stay inside these ranges and needn't reach their ends.
Inputs may be any that keep to these rules, and one draw needn't show every extreme that they name: `doc_ids`: each aligned group of 1024 slots holds whole sequences of 1 to 512 tokens with increasing ids, followed by padding slots marked -1; ids are never shared by two groups; at least half of a group's slots are live, and some group has no padding.
All inputs are finite; a program needn't handle non-finite values.
Results may differ from the reference program's by a relative error of at most 0.013.
The reference program's roundings to bfloat16 on the way count: a program that leaves them out, or rounds other values in their place, can miss the bound.
Values sent between devices are 32-bit elements; how exact they have to be, the bound alone decides.
A program may use at most 128 MiB of HBM per device.

```python
import jax
import jax.numpy as jnp
from jax import lax

D = 768
HEADS = 12
HD = 64
FF = 1152
HALF = 64
TOK_DEV = 1024
TOKENS = 8192


def draw_doc_ids(key, part):
    key = jax.random.fold_in(key, 11)
    key_flags, key_live, key_full, key_short = jax.random.split(key, 4)
    groups = TOKENS // TOK_DEV
    slot_index = jnp.arange(TOK_DEV, dtype=jnp.int32)
    flags = jax.random.randint(key_flags, (groups, TOK_DEV), 0, max(TOK_DEV // 3, 2)) == 0
    flags = flags | (slot_index[None, :] % 512 == 0)
    live = jax.random.randint(key_live, (groups,), TOK_DEV // 2, TOK_DEV + 1)
    full_group = jax.random.randint(key_full, (), 0, groups)
    short_group = (full_group + 1 + jax.random.randint(key_short, (), 0, max(groups - 1, 1))) % groups
    live = live.at[short_group].set(TOK_DEV // 2)
    live = live.at[full_group].set(TOK_DEV)
    is_live = slot_index[None, :] < live[:, None]
    live_flags = (flags & is_live).astype(jnp.int32)
    counted = jnp.cumsum(live_flags, axis=1) - 1
    flag_total = jnp.sum(live_flags, axis=1, keepdims=True)
    base = jnp.arange(groups, dtype=jnp.int32)[:, None] * TOK_DEV
    numbers = jnp.where(is_live, base + TOK_DEV - flag_total + counted, -1)
    return numbers.reshape(TOKENS).astype(jnp.int32)


def level_of(stream_key, dims, shards, low, largest):
    def one(axis_at, shards_of):
        steps = jax.random.uniform(jax.random.fold_in(jax.random.fold_in(stream_key, 6), axis_at), (shards_of,), jnp.float32, low / len(shards), largest / len(shards))
        return jnp.repeat(jnp.exp(steps), dims[axis_at] // shards_of).reshape((-1,) + (1,) * (len(dims) - axis_at - 1))

    factor_of = one(*shards[0])
    for cut in shards[1:]:
        factor_of = factor_of * one(*cut)
    return factor_of


def bell_draw(stream_key, extent, scale, reach, cuts=(), kind=jnp.bfloat16):
    values = scale * jax.random.normal(stream_key, extent, jnp.float32)
    if cuts:
        values = values * level_of(stream_key, extent, cuts, -0.22, 0.18)
    return jnp.clip(values, -reach, reach).astype(kind)


def setup_inputs(seed: int = 0) -> dict:
    streams_of = jax.random.split(jax.random.key(seed), 10)
    layer_in = bell_draw(streams_of[0], (TOKENS, D), 1.0, 6.0, ((0, 8),))
    doc_ids = draw_doc_ids(jax.random.fold_in(streams_of[9], 71), 0)
    qkv_weight = bell_draw(streams_of[2], (3, D, D), D ** -0.5, 0.21875, ((2, 4),))
    out_weight = bell_draw(streams_of[3], (D, D), (D // 32) ** -0.5, 1.25, ((0, 4),))
    up_weight = bell_draw(streams_of[4], (2, D, FF), D ** -0.5, 0.21875, ((2, 4),))
    down_weight = bell_draw(streams_of[5], (FF, D), (FF // 2) ** -0.5, 0.25, ((0, 4),))
    norm1_gain = jnp.clip(1.0 + 0.1 * jax.random.normal(streams_of[6], (D,), jnp.float32), 0.5, 1.5).astype(jnp.bfloat16)
    norm2_gain = jnp.clip(1.0 + 0.1 * jax.random.normal(streams_of[7], (D,), jnp.float32), 0.5, 1.5).astype(jnp.bfloat16)
    out_cotangent = bell_draw(streams_of[8], (TOKENS, D), 1.0, 6.0, ((0, 8),))
    return {"layer_in": layer_in, "doc_ids": doc_ids, "qkv_weight": qkv_weight, "out_weight": out_weight, "up_weight": up_weight, "down_weight": down_weight, "norm1_gain": norm1_gain, "norm2_gain": norm2_gain, "out_cotangent": out_cotangent}


@jax.custom_vjp
def low(v):
    return lax.optimization_barrier(v.astype(jnp.bfloat16)).astype(jnp.float32)

@jax.custom_vjp
def low_back(v):
    return v

def low_keep(v):
    return (low(v), None)

def low_pass(kept, grad):
    return (grad,)

def back_keep(v):
    return (v, None)

def back_low(kept, grad):
    return (low(grad),)
low.defvjp(low_keep, low_pass)
low_back.defvjp(back_keep, back_low)

def product(left, right):
    return jnp.dot(left, right, precision=lax.Precision.HIGHEST)

def layer_norm(values, gain):
    row_mean = lax.optimization_barrier(jnp.mean(values, axis=-1, keepdims=True))
    centred = values - row_mean
    variance = lax.optimization_barrier(jnp.mean(centred * centred, axis=-1, keepdims=True))
    return centred * lax.rsqrt(variance + 1e-05) * gain

def positions(doc_rows):
    row_length = doc_rows.shape[1]
    slot_index = jnp.arange(row_length, dtype=jnp.int32)
    previous = jnp.concatenate([doc_rows[:, :1] - 1, doc_rows[:, :-1]], axis=1)
    starts = jnp.where(doc_rows != previous, slot_index[None, :], 0).astype(jnp.int32)
    return slot_index[None, :] - lax.cummax(starts, axis=1)

def tables(places):
    half_dim = HD // 2
    freqs = 10000.0 ** (-jnp.arange(half_dim, dtype=jnp.float32) * 2.0 / HD)
    angles = places.astype(jnp.float32)[:, None] * freqs[None, :]
    angles = jnp.concatenate([angles, angles], axis=-1)
    return (jnp.cos(angles), jnp.sin(angles))

def rotate(values, cosine_table, sine_table):
    half_dim = values.shape[-1] // 2
    turned = jnp.concatenate([-values[..., half_dim:], values[..., :half_dim]], axis=-1)
    return values * cosine_table[:, None, :] + turned * sine_table[:, None, :]

def attend_block(pieces):
    query, keys_rot, values, allowed = pieces
    scores = jnp.einsum('qhd,khd->hqk', query, keys_rot, precision=lax.Precision.HIGHEST) * HD ** (-0.5)
    scores = low_back(scores)
    scores = jnp.where(allowed[None], scores, -1e+30)
    probs = low(jax.nn.softmax(scores, axis=-1))
    return jnp.einsum('hqk,khd->qhd', probs, values, precision=lax.Precision.HIGHEST)

def reference(layer_in, doc_ids, qkv_weight, out_weight, up_weight, down_weight, norm1_gain, norm2_gain, out_cotangent):
    groups = TOKENS // TOK_DEV
    doc_rows = doc_ids.reshape(groups, TOK_DEV)
    places = positions(doc_rows).reshape(TOKENS)
    cosine_table, sine_table = tables(places)
    slot_index = jnp.arange(TOK_DEV, dtype=jnp.int32)
    distance = jnp.abs(slot_index[:, None] - slot_index[None, :])
    same_doc = (doc_rows[:, :, None] == doc_rows[:, None, :]) & (doc_rows[:, :, None] >= 0)
    allowed = same_doc & (distance <= HALF)[None] | (distance == 0)[None]

    def to_groups(array):
        return array.reshape(groups, TOK_DEV, HEADS, HD)

    def forward(layer_float, qkv_float, out_float, up_float, down_float, gain_one, gain_two):
        hidden_one = low(layer_norm(layer_float, gain_one))
        query_proj = low_back(product(hidden_one, qkv_float[0]))
        key_proj = low_back(product(hidden_one, qkv_float[1]))
        value_proj = low_back(product(hidden_one, qkv_float[2]))
        query = low(rotate(query_proj.reshape(TOKENS, HEADS, HD), cosine_table, sine_table))
        keys_rot = low(rotate(key_proj.reshape(TOKENS, HEADS, HD), cosine_table, sine_table))
        values = low(value_proj.reshape(TOKENS, HEADS, HD))
        attended = lax.map(jax.checkpoint(attend_block), (to_groups(query), to_groups(keys_rot), to_groups(values), allowed))
        attended = low(low_back(attended.reshape(TOKENS, D)))
        attn_branch = low_back(product(attended, out_float))
        middle = layer_float + attn_branch
        hidden_two = low(layer_norm(middle, gain_two))
        gate_in = low_back(product(hidden_two, up_float[0]))
        gate_up = low_back(product(hidden_two, up_float[1]))
        activated = low(jax.nn.gelu(gate_in, approximate=False) * gate_up)
        return middle + low_back(product(activated, down_float))
    layer_out, pull = jax.vjp(forward, layer_in.astype(jnp.float32), qkv_weight.astype(jnp.float32), out_weight.astype(jnp.float32), up_weight.astype(jnp.float32), down_weight.astype(jnp.float32), norm1_gain.astype(jnp.float32), norm2_gain.astype(jnp.float32))
    grads = pull(out_cotangent.astype(jnp.float32))
    return (layer_out.astype(jnp.bfloat16), grads[0].astype(jnp.bfloat16), grads[1], grads[2], grads[3], grads[4], grads[5], grads[6])
```

```python
import functools

import jax
import jax.numpy as jnp
from jax import lax
from jax.sharding import PartitionSpec as P

HD = 64
HALF = 64


def layer_norm(values, gain):
    row_mean = jnp.mean(values, axis=-1, keepdims=True)
    centred = values - row_mean
    variance = jnp.mean(centred * centred, axis=-1, keepdims=True)
    return centred * lax.rsqrt(variance + 1e-05) * gain


def exact_gelu(values):
    return jax.nn.gelu(values, approximate=False)


def tables(places):
    half_dim = HD // 2
    freqs = 10000.0 ** (-jnp.arange(half_dim, dtype=jnp.float32) * 2.0 / HD)
    angles = places.astype(jnp.float32)[:, None] * freqs[None, :]
    angles = jnp.concatenate([angles, angles], axis=-1)
    return (jnp.cos(angles), jnp.sin(angles))


def rotate(values, cosine_table, sine_table):
    half_dim = values.shape[-1] // 2
    turned = jnp.concatenate([-values[..., half_dim:], values[..., :half_dim]], axis=-1)
    return values * cosine_table[:, None, :] + turned * sine_table[:, None, :]


def window(array, block, fill):
    blocks = array.shape[0] // block
    widths = [(block, block)] + [(0, 0)] * (array.ndim - 1)
    padded = jnp.pad(array, widths, constant_values=fill)
    shaped = padded.reshape((blocks + 2, block) + array.shape[1:])
    return jnp.concatenate([shaped[:-2], shaped[1:-1], shaped[2:]], axis=1)


def fold_window(pieces, block):
    blocks = pieces.shape[0]
    rest = [(0, 0)] * (pieces.ndim - 1)
    middle_part = pieces[:, block : 2 * block]
    from_before = jnp.pad(pieces[:-1, 2 * block :], [(1, 0)] + rest)
    from_after = jnp.pad(pieces[1:, :block], [(0, 1)] + rest)
    whole = middle_part + from_before + from_after
    return whole.reshape((blocks * block,) + pieces.shape[2:])


def masked_scores(query_blocks, key_window, allowed):
    scores = jnp.einsum(
        "nqhd,nkhd->nhqk", query_blocks, key_window, preferred_element_type=jnp.float32
    ) * HD ** (-0.5)
    return jnp.where(allowed[:, None], scores, -1e30)


def swap(array, axis, mask, size):
    return lax.ppermute(array, axis, [(i, i ^ mask) for i in range(size)])


def halve(array):
    return array * 0.5


def rows_of(array, part, rows):
    return lax.dynamic_slice_in_dim(array, part * rows, rows, axis=0)


def place_two(mine, other, bit):
    both = jnp.zeros((2,) + mine.shape, mine.dtype)
    both = lax.dynamic_update_index_in_dim(both, mine, bit, 0)
    return lax.dynamic_update_index_in_dim(both, other, 1 - bit, 0)


def halving_sum(buffer, me, masks, size):
    for mask in masks:
        bit = (me // mask) % 2
        half = buffer.shape[0] // 2
        sent = rows_of(buffer, 1 - bit, half)
        kept = rows_of(buffer, bit, half)
        buffer = kept + swap(sent, "dp", mask, size)
    for mask in reversed(masks):
        bit = (me // mask) % 2
        other = swap(buffer, "dp", mask, size)
        buffer = place_two(buffer, other, bit).reshape((-1,) + buffer.shape[1:])
    return buffer


def dp_sum(pieces, me, size):
    rows = sum(piece.shape[0] for piece in pieces)
    unit = 16 * size
    padded = -(-rows // unit) * unit
    if padded > rows:
        pieces = list(pieces) + [jnp.zeros((padded - rows, pieces[0].shape[1]), jnp.float32)]
    whole = jnp.concatenate(pieces, axis=0)
    masks = []
    mask = 1
    while mask < size:
        masks.append(mask)
        mask *= 2
    cut = padded // 2
    first = halving_sum(whole[:cut], me, masks, size)
    second = halving_sum(whole[cut:], me, masks[1:] + masks[:1], size)
    return jnp.concatenate([first, second], axis=0)[:rows]


def per_device(
    tensor_size,
    dp_size,
    layer_in,
    doc_ids,
    qkv_weight,
    out_weight,
    up_weight,
    down_weight,
    norm1_gain,
    norm2_gain,
    out_cotangent,
):
    token_rows, width = layer_in.shape
    heads_local = qkv_weight.shape[2] // HD
    columns = heads_local * HD
    block = 2 * HALF
    blocks = token_rows // block
    half_rows = token_rows // 2
    lane = lax.axis_index("tensor")
    me = lax.axis_index("dp")
    core = lane % 2
    bfloat = jnp.bfloat16
    float32 = jnp.float32

    def across(array, mask):
        return swap(array, "tensor", mask, tensor_size)

    weight_float = out_weight.astype(float32) * 2.0
    weight_two = across(weight_float, 2)
    weight_one = across(weight_float, 1)
    weight_three = across(weight_two, 1)
    out_full = jnp.zeros((tensor_size,) + out_weight.shape, bfloat)
    out_full = lax.dynamic_update_index_in_dim(out_full, out_weight, lane, 0)
    for mask, piece in ((1, weight_one), (2, weight_two), (3, weight_three)):
        out_full = lax.dynamic_update_index_in_dim(
            out_full, halve(piece).astype(bfloat), lane ^ mask, 0
        )

    slot_index = jnp.arange(token_rows, dtype=jnp.int32)
    previous = jnp.concatenate([doc_ids[:1] - 1, doc_ids[:-1]])
    starts = jnp.where(doc_ids != previous, slot_index, 0)
    places = slot_index - lax.cummax(starts, axis=0)
    cosine_table, sine_table = tables(places)
    query_slots = slot_index.reshape(blocks, block)
    key_slots = (
        jnp.arange(blocks, dtype=jnp.int32)[:, None] * block
        - block
        + jnp.arange(3 * block, dtype=jnp.int32)[None, :]
    )
    query_docs = doc_ids.reshape(blocks, block)
    key_docs = window(doc_ids, block, -2)
    distance = jnp.abs(query_slots[:, :, None] - key_slots[:, None, :])
    same_doc = (query_docs[:, :, None] == key_docs[:, None, :]) & (query_docs[:, :, None] >= 0)
    allowed = same_doc & (distance <= HALF) | (distance == 0)

    def turn(values):
        return rotate(values.reshape(token_rows, heads_local, HD), cosine_table, sine_table)

    gain_one = norm1_gain.astype(float32)
    gain_two = norm2_gain.astype(float32)
    layer_float = layer_in.astype(float32)
    hidden_one = layer_norm(layer_float, gain_one).astype(bfloat)
    projected = jnp.einsum("td,cde->cte", hidden_one, qkv_weight, preferred_element_type=float32)
    query_float, query_pull = jax.vjp(turn, projected[0])
    key_float, key_pull = jax.vjp(turn, projected[1])
    query = query_float.astype(bfloat)
    keys_rot = key_float.astype(bfloat)
    values = projected[2].reshape(token_rows, heads_local, HD).astype(bfloat)
    query_blocks = query.reshape(blocks, block, heads_local, HD)
    key_window = window(keys_rot, block, 0)
    value_window = window(values, block, 0)
    scores = masked_scores(query_blocks, key_window, allowed)
    top_score = jnp.max(scores, axis=-1, keepdims=True)
    expo = jnp.exp(scores - top_score)
    total = jnp.sum(expo, axis=-1, keepdims=True)
    probs = expo / total
    log_total = top_score + jnp.log(total)
    attended = jnp.einsum(
        "nhqk,nkhd->nqhd", probs.astype(bfloat), value_window, preferred_element_type=float32
    )
    attended_float = attended.reshape(token_rows, columns)
    attended = attended_float.astype(bfloat)

    attended_mine = rows_of(attended, core, half_rows)
    doubled = attended_float * 2.0
    float_mine = rows_of(doubled, core, half_rows)
    float_other = rows_of(doubled, 1 - core, half_rows)
    from_three = across(float_other, 3)
    from_two = across(float_mine, 2)
    from_one = across(float_other, 1)
    all_heads = jnp.zeros((tensor_size, half_rows, columns), bfloat)
    all_heads = lax.dynamic_update_index_in_dim(all_heads, attended_mine, lane, 0)
    for mask, piece in ((1, from_one), (2, from_two), (3, from_three)):
        all_heads = lax.dynamic_update_index_in_dim(
            all_heads, halve(piece).astype(bfloat), lane ^ mask, 0
        )
    attn_branch = jnp.einsum("jte,jed->td", all_heads, out_full, preferred_element_type=float32)
    layer_mine = rows_of(layer_float, core, half_rows)
    layer_other = rows_of(layer_float, 1 - core, half_rows)
    middle = layer_mine + attn_branch
    norm_two_pull = jax.vjp(lambda rows: layer_norm(rows, gain_two), middle)[1]
    normed_two = layer_norm(middle, 1.0)
    hidden_mine = (normed_two * gain_two).astype(bfloat)
    hidden_other = (across(normed_two, 1) * gain_two).astype(bfloat)
    hidden_two = place_two(hidden_mine, hidden_other, core).reshape(token_rows, width)

    up_parts = jnp.einsum("td,cdf->ctf", hidden_two, up_weight, preferred_element_type=float32)
    gate_in = up_parts[0]
    gate_up = up_parts[1]
    gelu_value, gelu_pull = jax.vjp(exact_gelu, gate_in)
    activated = (gelu_value * gate_up).astype(bfloat)
    grad_act = jnp.einsum("td,fd->tf", out_cotangent, down_weight, preferred_element_type=float32)
    grad_gate_in = gelu_pull(grad_act * gate_up)[0]
    grad_gate_up = grad_act * gelu_value
    grad_up_parts = jnp.stack([grad_gate_in, grad_gate_up], axis=1).astype(bfloat)

    def tensor_sum(product, rows_in):
        part_other = product(rows_of(rows_in, 1 - core, half_rows))
        arrived = across(part_other, 1)
        part_mine = product(rows_of(rows_in, core, half_rows))
        mine = part_mine + arrived
        return mine + across(mine, 2)

    grad_hidden_two = tensor_sum(
        lambda rows: jnp.einsum("tcf,cdf->td", rows, up_weight, preferred_element_type=float32),
        grad_up_parts,
    )
    cot_mine = rows_of(out_cotangent, core, half_rows).astype(float32)
    cot_other = rows_of(out_cotangent, 1 - core, half_rows).astype(float32)
    norm_two_part = norm_two_pull(grad_hidden_two)[0]
    branch_mine = (cot_mine + norm_two_part).astype(bfloat)
    branch_other = (cot_other + across(norm_two_part, 1)).astype(bfloat)
    grad_branch = place_two(branch_mine, branch_other, core).reshape(token_rows, width)

    mlp_branch = tensor_sum(
        lambda rows: jnp.dot(rows, down_weight, preferred_element_type=float32), activated
    )
    both_branches = attn_branch + mlp_branch
    out_mine = (layer_mine + both_branches).astype(bfloat)
    out_other = (layer_other + across(both_branches, 1)).astype(bfloat)
    layer_out = place_two(out_mine, out_other, core).reshape(token_rows, width)

    grad_down = jnp.einsum("tf,td->fd", activated, out_cotangent, preferred_element_type=float32)
    grad_up = jnp.einsum("td,tcf->cfd", hidden_two, grad_up_parts, preferred_element_type=float32)
    units = grad_down.shape[0]
    gain_grad_two = jnp.einsum("cfd,cdf->d", grad_up, up_weight.astype(float32)) / gain_two

    grad_out = jnp.einsum("te,td->ed", attended, grad_branch, preferred_element_type=float32)
    grad_attended = jnp.einsum("td,ed->te", grad_branch, out_weight, preferred_element_type=float32)
    grad_attended = grad_attended.reshape(blocks, block, heads_local, HD).astype(bfloat)
    probs_again = jnp.exp(masked_scores(query_blocks, key_window, allowed) - log_total)
    grad_value_window = jnp.einsum(
        "nhqk,nqhd->nkhd", probs_again.astype(bfloat), grad_attended, preferred_element_type=float32
    )
    grad_probs = jnp.einsum(
        "nqhd,nkhd->nhqk", grad_attended, value_window, preferred_element_type=float32
    )
    grad_scores = probs_again * (
        grad_probs - jnp.sum(probs_again * grad_probs, axis=-1, keepdims=True)
    )
    grad_scores = grad_scores.astype(bfloat)
    grad_query = jnp.einsum(
        "nhqk,nkhd->nqhd", grad_scores, key_window, preferred_element_type=float32
    ) * HD ** (-0.5)
    grad_key_window = jnp.einsum(
        "nhqk,nqhd->nkhd", grad_scores, query_blocks, preferred_element_type=float32
    ) * HD ** (-0.5)
    grad_query = grad_query.reshape(token_rows, heads_local, HD)
    grad_keys = fold_window(grad_key_window, block)
    grad_values = fold_window(grad_value_window, block)
    grad_query_proj = query_pull(grad_query)[0]
    grad_key_proj = key_pull(grad_keys)[0]
    grad_value_proj = grad_values.reshape(token_rows, -1)
    grad_projected = jnp.stack([grad_query_proj, grad_key_proj, grad_value_proj], axis=1).astype(
        bfloat
    )
    grad_hidden_one = tensor_sum(
        lambda rows: jnp.einsum("tce,cde->td", rows, qkv_weight, preferred_element_type=float32),
        grad_projected,
    )
    grad_qkv = jnp.einsum(
        "td,tce->ced", hidden_one, grad_projected, preferred_element_type=float32
    )
    gain_grad_one = jnp.einsum("ced,cde->d", grad_qkv, qkv_weight.astype(float32)) / gain_one
    gains = jnp.stack([gain_grad_one, gain_grad_two])
    for mask in (1, 2):
        gains = gains + across(gains, mask)
    mask = 1
    while mask < dp_size:
        gains = gains + swap(gains, "dp", mask, dp_size)
        mask *= 2

    norm_one_pull = jax.vjp(lambda rows: layer_norm(rows, gain_one), layer_mine)[1]
    both_norms = norm_two_part + norm_one_pull(grad_hidden_one)[0]
    input_mine = (cot_mine + both_norms).astype(bfloat)
    input_other = (cot_other + across(both_norms, 1)).astype(bfloat)
    input_grad = place_two(input_mine, input_other, core).reshape(token_rows, width)

    early = dp_sum([grad_up.reshape(2 * units, width), grad_down, grad_out], me, dp_size)
    late = dp_sum([grad_qkv.reshape(3 * columns, width)], me, dp_size)
    grad_up = early[: 2 * units].reshape(2, units, width).transpose(0, 2, 1)
    grad_down = early[2 * units : 3 * units]
    grad_out = early[3 * units :]
    grad_qkv = late.reshape(3, columns, width).transpose(0, 2, 1)
    return (layer_out, input_grad, grad_qkv, grad_out, grad_up, grad_down, gains[0], gains[1])


def solution(mesh):
    return jax.shard_map(
        functools.partial(per_device, mesh.shape["tensor"], mesh.shape["dp"]),
        mesh=mesh,
        in_specs=(
            P("dp", None),
            P("dp"),
            P(None, None, "tensor"),
            P("tensor", None),
            P(None, None, "tensor"),
            P("tensor", None),
            P(),
            P(),
            P("dp", None),
        ),
        out_specs=(
            P("dp", None),
            P("dp", None),
            P(None, None, "tensor"),
            P("tensor", None),
            P(None, None, "tensor"),
            P("tensor", None),
            P(),
            P(),
        ),
        check_vma=False,
    )
```

```python
import functools

import jax
import jax.numpy as jnp
from jax import lax
from jax.sharding import PartitionSpec as P

HD = 64
HALF = 64


def layer_norm(values, gain):
    row_mean = jnp.mean(values, axis=-1, keepdims=True)
    centred = values - row_mean
    variance = jnp.mean(centred * centred, axis=-1, keepdims=True)
    return centred * lax.rsqrt(variance + 1e-05) * gain


def exact_gelu(values):
    return jax.nn.gelu(values, approximate=False)


def tables(places):
    half_dim = HD // 2
    freqs = 10000.0 ** (-jnp.arange(half_dim, dtype=jnp.float32) * 2.0 / HD)
    angles = places.astype(jnp.float32)[:, None] * freqs[None, :]
    angles = jnp.concatenate([angles, angles], axis=-1)
    return (jnp.cos(angles), jnp.sin(angles))


def rotate(values, cosine_table, sine_table):
    half_dim = values.shape[-1] // 2
    turned = jnp.concatenate([-values[..., half_dim:], values[..., :half_dim]], axis=-1)
    return values * cosine_table[:, None, :] + turned * sine_table[:, None, :]


def window(array, block, fill):
    blocks = array.shape[0] // block
    widths = [(block, block)] + [(0, 0)] * (array.ndim - 1)
    padded = jnp.pad(array, widths, constant_values=fill)
    shaped = padded.reshape((blocks + 2, block) + array.shape[1:])
    return jnp.concatenate([shaped[:-2], shaped[1:-1], shaped[2:]], axis=1)


def fold_window(pieces, block):
    blocks = pieces.shape[0]
    rest = [(0, 0)] * (pieces.ndim - 1)
    middle_part = pieces[:, block : 2 * block]
    from_before = jnp.pad(pieces[:-1, 2 * block :], [(1, 0)] + rest)
    from_after = jnp.pad(pieces[1:, :block], [(0, 1)] + rest)
    whole = middle_part + from_before + from_after
    return whole.reshape((blocks * block,) + pieces.shape[2:])


def masked_scores(query_blocks, key_window, allowed):
    scores = jnp.einsum(
        "nqhd,nkhd->nhqk", query_blocks, key_window, preferred_element_type=jnp.float32
    ) * HD ** (-0.5)
    return jnp.where(allowed[:, None], scores, -1e30)


def swap(array, axis, mask, size):
    return lax.ppermute(array, axis, [(i, i ^ mask) for i in range(size)])


def halve(array):
    return array * 0.5


def rows_of(array, part, rows):
    return lax.dynamic_slice_in_dim(array, part * rows, rows, axis=0)


def place_two(mine, other, bit):
    both = jnp.zeros((2,) + mine.shape, mine.dtype)
    both = lax.dynamic_update_index_in_dim(both, mine, bit, 0)
    return lax.dynamic_update_index_in_dim(both, other, 1 - bit, 0)


def per_device(
    tensor_size,
    dp_size,
    layer_in,
    doc_ids,
    qkv_weight,
    out_weight,
    up_weight,
    down_weight,
    norm1_gain,
    norm2_gain,
    out_cotangent,
):
    token_rows, width = layer_in.shape
    heads_local = qkv_weight.shape[2] // HD
    columns = heads_local * HD
    block = 2 * HALF
    blocks = token_rows // block
    half_rows = token_rows // 2
    lane = lax.axis_index("tensor")
    me = lax.axis_index("dp")
    core = lane % 2
    bfloat = jnp.bfloat16
    float32 = jnp.float32

    def across(array, mask):
        return swap(array, "tensor", mask, tensor_size)

    weight_float = out_weight.astype(float32) * 2.0
    weight_two = across(weight_float, 2)
    weight_one = across(weight_float, 1)
    weight_three = across(weight_two, 1)
    out_full = jnp.zeros((tensor_size,) + out_weight.shape, bfloat)
    out_full = lax.dynamic_update_index_in_dim(out_full, out_weight, lane, 0)
    for mask, piece in ((1, weight_one), (2, weight_two), (3, weight_three)):
        out_full = lax.dynamic_update_index_in_dim(
            out_full, halve(piece).astype(bfloat), lane ^ mask, 0
        )

    slot_index = jnp.arange(token_rows, dtype=jnp.int32)
    previous = jnp.concatenate([doc_ids[:1] - 1, doc_ids[:-1]])
    starts = jnp.where(doc_ids != previous, slot_index, 0)
    places = slot_index - lax.cummax(starts, axis=0)
    cosine_table, sine_table = tables(places)
    query_slots = slot_index.reshape(blocks, block)
    key_slots = (
        jnp.arange(blocks, dtype=jnp.int32)[:, None] * block
        - block
        + jnp.arange(3 * block, dtype=jnp.int32)[None, :]
    )
    query_docs = doc_ids.reshape(blocks, block)
    key_docs = window(doc_ids, block, -2)
    distance = jnp.abs(query_slots[:, :, None] - key_slots[:, None, :])
    same_doc = (query_docs[:, :, None] == key_docs[:, None, :]) & (query_docs[:, :, None] >= 0)
    allowed = same_doc & (distance <= HALF) | (distance == 0)

    def turn(values):
        return rotate(values.reshape(token_rows, heads_local, HD), cosine_table, sine_table)

    gain_one = norm1_gain.astype(float32)
    gain_two = norm2_gain.astype(float32)
    layer_float = layer_in.astype(float32)
    hidden_one = layer_norm(layer_float, gain_one).astype(bfloat)
    projected = jnp.einsum("td,cde->cte", hidden_one, qkv_weight, preferred_element_type=float32)
    query_float, query_pull = jax.vjp(turn, projected[0])
    key_float, key_pull = jax.vjp(turn, projected[1])
    query = query_float.astype(bfloat)
    keys_rot = key_float.astype(bfloat)
    values = projected[2].reshape(token_rows, heads_local, HD).astype(bfloat)
    query_blocks = query.reshape(blocks, block, heads_local, HD)
    key_window = window(keys_rot, block, 0)
    value_window = window(values, block, 0)
    scores = masked_scores(query_blocks, key_window, allowed)
    top_score = jnp.max(scores, axis=-1, keepdims=True)
    expo = jnp.exp(scores - top_score)
    total = jnp.sum(expo, axis=-1, keepdims=True)
    probs = expo / total
    log_total = top_score + jnp.log(total)
    attended = jnp.einsum(
        "nhqk,nkhd->nqhd", probs.astype(bfloat), value_window, preferred_element_type=float32
    )
    attended_float = attended.reshape(token_rows, columns)
    attended = attended_float.astype(bfloat)

    attended_mine = rows_of(attended, core, half_rows)
    doubled = attended_float * 2.0
    float_mine = rows_of(doubled, core, half_rows)
    float_other = rows_of(doubled, 1 - core, half_rows)
    from_three = across(float_other, 3)
    from_two = across(float_mine, 2)
    from_one = across(float_other, 1)
    all_heads = jnp.zeros((tensor_size, half_rows, columns), bfloat)
    all_heads = lax.dynamic_update_index_in_dim(all_heads, attended_mine, lane, 0)
    for mask, piece in ((1, from_one), (2, from_two), (3, from_three)):
        all_heads = lax.dynamic_update_index_in_dim(
            all_heads, halve(piece).astype(bfloat), lane ^ mask, 0
        )
    attn_branch = jnp.einsum("jte,jed->td", all_heads, out_full, preferred_element_type=float32)
    layer_mine = rows_of(layer_float, core, half_rows)
    layer_other = rows_of(layer_float, 1 - core, half_rows)
    middle = layer_mine + attn_branch
    norm_two_pull = jax.vjp(lambda rows: layer_norm(rows, gain_two), middle)[1]
    normed_two = layer_norm(middle, 1.0)
    hidden_mine = (normed_two * gain_two).astype(bfloat)
    hidden_other = (across(normed_two, 1) * gain_two).astype(bfloat)
    hidden_two = place_two(hidden_mine, hidden_other, core).reshape(token_rows, width)

    up_parts = jnp.einsum("td,cdf->ctf", hidden_two, up_weight, preferred_element_type=float32)
    gate_in = up_parts[0]
    gate_up = up_parts[1]
    gelu_value, gelu_pull = jax.vjp(exact_gelu, gate_in)
    activated = (gelu_value * gate_up).astype(bfloat)
    grad_act = jnp.einsum("td,fd->tf", out_cotangent, down_weight, preferred_element_type=float32)
    grad_gate_in = gelu_pull(grad_act * gate_up)[0]
    grad_gate_up = grad_act * gelu_value
    grad_up_parts = jnp.stack([grad_gate_in, grad_gate_up], axis=1).astype(bfloat)

    def tensor_sum(product, rows_in):
        part_other = product(rows_of(rows_in, 1 - core, half_rows))
        arrived = across(part_other, 1)
        part_mine = product(rows_of(rows_in, core, half_rows))
        mine = part_mine + arrived
        return mine + across(mine, 2)

    grad_hidden_two = tensor_sum(
        lambda rows: jnp.einsum("tcf,cdf->td", rows, up_weight, preferred_element_type=float32),
        grad_up_parts,
    )
    cot_mine = rows_of(out_cotangent, core, half_rows).astype(float32)
    cot_other = rows_of(out_cotangent, 1 - core, half_rows).astype(float32)
    norm_two_part = norm_two_pull(grad_hidden_two)[0]
    branch_mine = (cot_mine + norm_two_part).astype(bfloat)
    branch_other = (cot_other + across(norm_two_part, 1)).astype(bfloat)
    grad_branch = place_two(branch_mine, branch_other, core).reshape(token_rows, width)

    mlp_branch = tensor_sum(
        lambda rows: jnp.dot(rows, down_weight, preferred_element_type=float32), activated
    )
    both_branches = attn_branch + mlp_branch
    out_mine = (layer_mine + both_branches).astype(bfloat)
    out_other = (layer_other + across(both_branches, 1)).astype(bfloat)
    layer_out = place_two(out_mine, out_other, core).reshape(token_rows, width)

    grad_down = jnp.einsum("tf,td->fd", activated, out_cotangent, preferred_element_type=float32)
    grad_up = jnp.einsum("td,tcf->cfd", hidden_two, grad_up_parts, preferred_element_type=float32)
    gain_grad_two = jnp.einsum("cfd,cdf->d", grad_up, up_weight.astype(float32)) / gain_two

    grad_out = jnp.einsum("te,td->ed", attended, grad_branch, preferred_element_type=float32)
    grad_attended = jnp.einsum("td,ed->te", grad_branch, out_weight, preferred_element_type=float32)
    grad_attended = grad_attended.reshape(blocks, block, heads_local, HD).astype(bfloat)
    probs_again = jnp.exp(masked_scores(query_blocks, key_window, allowed) - log_total)
    grad_value_window = jnp.einsum(
        "nhqk,nqhd->nkhd", probs_again.astype(bfloat), grad_attended, preferred_element_type=float32
    )
    grad_probs = jnp.einsum(
        "nqhd,nkhd->nhqk", grad_attended, value_window, preferred_element_type=float32
    )
    grad_scores = probs_again * (
        grad_probs - jnp.sum(probs_again * grad_probs, axis=-1, keepdims=True)
    )
    grad_scores = grad_scores.astype(bfloat)
    grad_query = jnp.einsum(
        "nhqk,nkhd->nqhd", grad_scores, key_window, preferred_element_type=float32
    ) * HD ** (-0.5)
    grad_key_window = jnp.einsum(
        "nhqk,nqhd->nkhd", grad_scores, query_blocks, preferred_element_type=float32
    ) * HD ** (-0.5)
    grad_query = grad_query.reshape(token_rows, heads_local, HD)
    grad_keys = fold_window(grad_key_window, block)
    grad_values = fold_window(grad_value_window, block)
    grad_query_proj = query_pull(grad_query)[0]
    grad_key_proj = key_pull(grad_keys)[0]
    grad_value_proj = grad_values.reshape(token_rows, -1)
    grad_projected = jnp.stack([grad_query_proj, grad_key_proj, grad_value_proj], axis=1).astype(
        bfloat
    )
    grad_hidden_one = tensor_sum(
        lambda rows: jnp.einsum("tce,cde->td", rows, qkv_weight, preferred_element_type=float32),
        grad_projected,
    )
    grad_qkv = jnp.einsum(
        "td,tce->ced", hidden_one, grad_projected, preferred_element_type=float32
    )
    gain_grad_one = jnp.einsum("ced,cde->d", grad_qkv, qkv_weight.astype(float32)) / gain_one
    gains = jnp.stack([gain_grad_one, gain_grad_two])
    for mask in (1, 2):
        gains = gains + across(gains, mask)
    mask = 1
    while mask < dp_size:
        gains = gains + swap(gains, "dp", mask, dp_size)
        mask *= 2

    norm_one_pull = jax.vjp(lambda rows: layer_norm(rows, gain_one), layer_mine)[1]
    both_norms = norm_two_part + norm_one_pull(grad_hidden_one)[0]
    input_mine = (cot_mine + both_norms).astype(bfloat)
    input_other = (cot_other + across(both_norms, 1)).astype(bfloat)
    input_grad = place_two(input_mine, input_other, core).reshape(token_rows, width)

    grad_up, grad_down = lax.psum((grad_up, grad_down), "dp")
    grad_qkv, grad_out, grad_up, grad_down = lax.optimization_barrier(
        (grad_qkv, grad_out, grad_up, grad_down)
    )
    grad_qkv, grad_out = lax.psum((grad_qkv, grad_out), "dp")
    grad_up = grad_up.transpose(0, 2, 1)
    grad_qkv = grad_qkv.transpose(0, 2, 1)
    return (layer_out, input_grad, grad_qkv, grad_out, grad_up, grad_down, gains[0], gains[1])


def solution(mesh):
    return jax.shard_map(
        functools.partial(per_device, mesh.shape["tensor"], mesh.shape["dp"]),
        mesh=mesh,
        in_specs=(
            P("dp", None),
            P("dp"),
            P(None, None, "tensor"),
            P("tensor", None),
            P(None, None, "tensor"),
            P("tensor", None),
            P(),
            P(),
            P("dp", None),
        ),
        out_specs=(
            P("dp", None),
            P("dp", None),
            P(None, None, "tensor"),
            P("tensor", None),
            P(None, None, "tensor"),
            P("tensor", None),
            P(),
            P(),
        ),
        check_vma=False,
    )
```

```python
import functools

import jax
import jax.numpy as jnp
from jax import lax
from jax.experimental import pallas as pl
from jax.experimental.pallas import tpu as pltpu
from jax.sharding import PartitionSpec as P

HD = 64
HALF = 64


def layer_norm(values, gain):
    row_mean = jnp.mean(values, axis=-1, keepdims=True)
    centred = values - row_mean
    variance = jnp.mean(centred * centred, axis=-1, keepdims=True)
    return centred * lax.rsqrt(variance + 1e-05) * gain


def exact_gelu(values):
    return jax.nn.gelu(values, approximate=False)


def tables(places):
    half_dim = HD // 2
    freqs = 10000.0 ** (-jnp.arange(half_dim, dtype=jnp.float32) * 2.0 / HD)
    angles = places.astype(jnp.float32)[:, None] * freqs[None, :]
    angles = jnp.concatenate([angles, angles], axis=-1)
    return (jnp.cos(angles), jnp.sin(angles))


def rotate(values, cosine_table, sine_table):
    half_dim = values.shape[-1] // 2
    turned = jnp.concatenate([-values[..., half_dim:], values[..., :half_dim]], axis=-1)
    return values * cosine_table[:, None, :] + turned * sine_table[:, None, :]


def window(array, block, fill):
    blocks = array.shape[0] // block
    widths = [(block, block)] + [(0, 0)] * (array.ndim - 1)
    padded = jnp.pad(array, widths, constant_values=fill)
    shaped = padded.reshape((blocks + 2, block) + array.shape[1:])
    return jnp.concatenate([shaped[:-2], shaped[1:-1], shaped[2:]], axis=1)


def fold_window(pieces, block):
    blocks = pieces.shape[0]
    rest = [(0, 0)] * (pieces.ndim - 1)
    middle_part = pieces[:, block : 2 * block]
    from_before = jnp.pad(pieces[:-1, 2 * block :], [(1, 0)] + rest)
    from_after = jnp.pad(pieces[1:, :block], [(0, 1)] + rest)
    whole = middle_part + from_before + from_after
    return whole.reshape((blocks * block,) + pieces.shape[2:])


def masked_scores(query_blocks, key_window, allowed):
    scores = jnp.einsum(
        "nqhd,nkhd->nhqk", query_blocks, key_window, preferred_element_type=jnp.float32
    ) * HD ** (-0.5)
    return jnp.where(allowed[:, None], scores, -1e30)


def swap(array, axis, mask, size):
    return lax.ppermute(array, axis, [(i, i ^ mask) for i in range(size)])


def halve(array):
    return array * 0.5


def rows_of(array, part, rows):
    return lax.dynamic_slice_in_dim(array, part * rows, rows, axis=0)


def place_two(mine, other, bit):
    both = jnp.zeros((2,) + mine.shape, mine.dtype)
    both = lax.dynamic_update_index_in_dim(both, mine, bit, 0)
    return lax.dynamic_update_index_in_dim(both, other, 1 - bit, 0)


def masks_of(size):
    masks = []
    mask = 1
    while mask < size:
        masks.append(mask)
        mask *= 2
    return masks


def late_kernel(dp_size, whole, gains, summed, gain_sum, kept, landed, gain_held, gain_landed, *sems):
    send_sem, recv_sem, back_send, back_recv, gain_send, gain_recv = sems
    me = lax.axis_index("dp")
    lane = lax.axis_index("tensor")
    masks = masks_of(dp_size)
    steps = len(masks)
    rows = whole.shape[0]
    half = rows // 2
    orders = (masks, masks[1:] + masks[:1])
    hops = [("tensor", 1), ("tensor", 2)] + [("dp", mask) for mask in masks]

    def flip(axis, mask):
        at = me if axis == "dp" else lane
        bit = (at // mask) % 2
        return {axis: at + mask * (1 - 2 * bit)}

    barrier = pltpu.get_barrier_semaphore()
    for axis, mask in hops:
        pl.semaphore_signal(
            barrier, inc=1, device_id=flip(axis, mask), device_id_type=pl.DeviceIdType.MESH
        )
    pl.semaphore_wait(barrier, len(hops))

    def span(start, size):
        return pl.ds(pl.multiple_of(start, 8), size)

    def gain_copy(step):
        return pltpu.make_async_remote_copy(
            src_ref=gain_held.at[step],
            dst_ref=gain_landed.at[step],
            send_sem=gain_send.at[step],
            recv_sem=gain_recv.at[step],
            device_id=flip(*hops[step]),
            device_id_type=pl.DeviceIdType.MESH,
        )

    def out_copy(chain, step, start, size):
        mask = orders[chain][step]
        bit = (me // mask) % 2
        base = chain * half + half - 2 * size
        source = whole if step == 0 else kept
        return pltpu.make_async_remote_copy(
            src_ref=source.at[span(start + (1 - bit) * size, size)],
            dst_ref=landed.at[pl.ds(base, size)],
            send_sem=send_sem.at[chain, step],
            recv_sem=recv_sem.at[chain, step],
            device_id=flip("dp", mask),
            device_id_type=pl.DeviceIdType.MESH,
        )

    def back_copy(chain, step, start, size):
        return pltpu.make_async_remote_copy(
            src_ref=summed.at[span(start, size)],
            dst_ref=summed.at[span(start, size)],
            send_sem=back_send.at[chain, step],
            recv_sem=back_recv.at[chain, step],
            device_id=flip("dp", orders[chain][step]),
            device_id_type=pl.DeviceIdType.MESH,
        )

    starts = [0, half]
    size = half // 2
    copies = [out_copy(chain, 0, starts[chain], size) for chain in range(2)]
    for copy in copies:
        copy.start()
    gain_held[0] = gains[...]
    gain_step = 0
    small = gain_copy(0)
    small.start()

    def advance_gains(small, step):
        small.wait()
        gain_held[step + 1] = gain_held[step] + gain_landed[step]
        if step + 1 < len(hops):
            small = gain_copy(step + 1)
            small.start()
        return small

    for step in range(steps):
        for chain in range(2):
            mask = orders[chain][step]
            bit = (me // mask) % 2
            copies[chain].wait()
            mine = span(starts[chain] + bit * size, size)
            base = chain * half + half - 2 * size
            source = whole if step == 0 else kept
            total = source[mine, :] + landed[pl.ds(base, size), :]
            starts[chain] = starts[chain] + bit * size
            if step + 1 < steps:
                kept[mine, :] = total
                copies[chain] = out_copy(chain, step + 1, starts[chain], size // 2)
            else:
                summed[mine, :] = total
                copies[chain] = back_copy(chain, step, starts[chain], size)
            copies[chain].start()
        if step + 1 < steps:
            size = size // 2
        if gain_step < len(hops):
            small = advance_gains(small, gain_step)
            gain_step += 1
    for step in reversed(range(steps)):
        for chain in range(2):
            copies[chain].wait()
            bit = (me // orders[chain][step]) % 2
            starts[chain] = starts[chain] - bit * size
            if step > 0:
                copies[chain] = back_copy(chain, step - 1, starts[chain], 2 * size)
                copies[chain].start()
        size = size * 2
        if gain_step < len(hops):
            small = advance_gains(small, gain_step)
            gain_step += 1
    gain_sum[...] = gain_held[len(hops)]


def late_sum(whole, gains, dp_size):
    steps = len(masks_of(dp_size))
    hops = steps + 2
    vmem = pl.BlockSpec(memory_space=pltpu.VMEM)
    return pl.pallas_call(
        functools.partial(late_kernel, dp_size),
        out_shape=(
            jax.ShapeDtypeStruct(whole.shape, jnp.float32),
            jax.ShapeDtypeStruct(gains.shape, jnp.float32),
        ),
        in_specs=[vmem, vmem],
        out_specs=(vmem, vmem),
        scratch_shapes=[
            pltpu.VMEM(whole.shape, jnp.float32),
            pltpu.VMEM(whole.shape, jnp.float32),
            pltpu.VMEM((hops + 1,) + gains.shape, jnp.float32),
            pltpu.VMEM((hops,) + gains.shape, jnp.float32),
            pltpu.SemaphoreType.DMA((2, steps)),
            pltpu.SemaphoreType.DMA((2, steps)),
            pltpu.SemaphoreType.DMA((2, steps)),
            pltpu.SemaphoreType.DMA((2, steps)),
            pltpu.SemaphoreType.DMA((hops,)),
            pltpu.SemaphoreType.DMA((hops,)),
        ],
        compiler_params=pltpu.CompilerParams(
            collective_id=0, has_side_effects=True, vmem_limit_bytes=32 * 1024 * 1024
        ),
        cost_estimate=pl.CostEstimate(flops=0, bytes_accessed=100000000, transcendentals=0),
    )(whole, gains)


def per_device(
    tensor_size,
    dp_size,
    layer_in,
    doc_ids,
    qkv_weight,
    out_weight,
    up_weight,
    down_weight,
    norm1_gain,
    norm2_gain,
    out_cotangent,
):
    token_rows, width = layer_in.shape
    heads_local = qkv_weight.shape[2] // HD
    columns = heads_local * HD
    block = 2 * HALF
    blocks = token_rows // block
    half_rows = token_rows // 2
    lane = lax.axis_index("tensor")
    me = lax.axis_index("dp")
    core = lane % 2
    bfloat = jnp.bfloat16
    float32 = jnp.float32

    def across(array, mask):
        return swap(array, "tensor", mask, tensor_size)

    weight_float = out_weight.astype(float32) * 2.0
    weight_two = across(weight_float, 2)
    weight_one = across(weight_float, 1)
    weight_three = across(weight_two, 1)
    out_full = jnp.zeros((tensor_size,) + out_weight.shape, bfloat)
    out_full = lax.dynamic_update_index_in_dim(out_full, out_weight, lane, 0)
    for mask, piece in ((1, weight_one), (2, weight_two), (3, weight_three)):
        out_full = lax.dynamic_update_index_in_dim(
            out_full, halve(piece).astype(bfloat), lane ^ mask, 0
        )

    slot_index = jnp.arange(token_rows, dtype=jnp.int32)
    previous = jnp.concatenate([doc_ids[:1] - 1, doc_ids[:-1]])
    starts = jnp.where(doc_ids != previous, slot_index, 0)
    places = slot_index - lax.cummax(starts, axis=0)
    cosine_table, sine_table = tables(places)
    query_slots = slot_index.reshape(blocks, block)
    key_slots = (
        jnp.arange(blocks, dtype=jnp.int32)[:, None] * block
        - block
        + jnp.arange(3 * block, dtype=jnp.int32)[None, :]
    )
    query_docs = doc_ids.reshape(blocks, block)
    key_docs = window(doc_ids, block, -2)
    distance = jnp.abs(query_slots[:, :, None] - key_slots[:, None, :])
    same_doc = (query_docs[:, :, None] == key_docs[:, None, :]) & (query_docs[:, :, None] >= 0)
    allowed = same_doc & (distance <= HALF) | (distance == 0)

    def turn(values):
        return rotate(values.reshape(token_rows, heads_local, HD), cosine_table, sine_table)

    gain_one = norm1_gain.astype(float32)
    gain_two = norm2_gain.astype(float32)
    layer_float = layer_in.astype(float32)
    hidden_one = layer_norm(layer_float, gain_one).astype(bfloat)
    projected = jnp.einsum("td,cde->cte", hidden_one, qkv_weight, preferred_element_type=float32)
    query_float, query_pull = jax.vjp(turn, projected[0])
    key_float, key_pull = jax.vjp(turn, projected[1])
    query = query_float.astype(bfloat)
    keys_rot = key_float.astype(bfloat)
    values = projected[2].reshape(token_rows, heads_local, HD).astype(bfloat)
    query_blocks = query.reshape(blocks, block, heads_local, HD)
    key_window = window(keys_rot, block, 0)
    value_window = window(values, block, 0)
    scores = masked_scores(query_blocks, key_window, allowed)
    top_score = jnp.max(scores, axis=-1, keepdims=True)
    expo = jnp.exp(scores - top_score)
    total = jnp.sum(expo, axis=-1, keepdims=True)
    probs = expo / total
    log_total = top_score + jnp.log(total)
    attended = jnp.einsum(
        "nhqk,nkhd->nqhd", probs.astype(bfloat), value_window, preferred_element_type=float32
    )
    attended_float = attended.reshape(token_rows, columns)
    attended = attended_float.astype(bfloat)

    attended_mine = rows_of(attended, core, half_rows)
    doubled = attended_float * 2.0
    float_mine = rows_of(doubled, core, half_rows)
    float_other = rows_of(doubled, 1 - core, half_rows)
    from_three = across(float_other, 3)
    from_two = across(float_mine, 2)
    from_one = across(float_other, 1)
    all_heads = jnp.zeros((tensor_size, half_rows, columns), bfloat)
    all_heads = lax.dynamic_update_index_in_dim(all_heads, attended_mine, lane, 0)
    for mask, piece in ((1, from_one), (2, from_two), (3, from_three)):
        all_heads = lax.dynamic_update_index_in_dim(
            all_heads, halve(piece).astype(bfloat), lane ^ mask, 0
        )
    attn_branch = jnp.einsum("jte,jed->td", all_heads, out_full, preferred_element_type=float32)
    layer_mine = rows_of(layer_float, core, half_rows)
    layer_other = rows_of(layer_float, 1 - core, half_rows)
    middle = layer_mine + attn_branch
    norm_two_pull = jax.vjp(lambda rows: layer_norm(rows, gain_two), middle)[1]
    normed_two = layer_norm(middle, 1.0)
    hidden_mine = (normed_two * gain_two).astype(bfloat)
    hidden_other = (across(normed_two, 1) * gain_two).astype(bfloat)
    hidden_two = place_two(hidden_mine, hidden_other, core).reshape(token_rows, width)

    up_parts = jnp.einsum("td,cdf->ctf", hidden_two, up_weight, preferred_element_type=float32)
    gate_in = up_parts[0]
    gate_up = up_parts[1]
    gelu_value, gelu_pull = jax.vjp(exact_gelu, gate_in)
    activated = (gelu_value * gate_up).astype(bfloat)
    grad_act = jnp.einsum("td,fd->tf", out_cotangent, down_weight, preferred_element_type=float32)
    grad_gate_in = gelu_pull(grad_act * gate_up)[0]
    grad_gate_up = grad_act * gelu_value
    grad_up_parts = jnp.stack([grad_gate_in, grad_gate_up], axis=1).astype(bfloat)

    def tensor_sum(product, rows_in):
        part_other = product(rows_of(rows_in, 1 - core, half_rows))
        arrived = across(part_other, 1)
        part_mine = product(rows_of(rows_in, core, half_rows))
        return part_mine + arrived

    hidden_two_half = tensor_sum(
        lambda rows: jnp.einsum("tcf,cdf->td", rows, up_weight, preferred_element_type=float32),
        grad_up_parts,
    )
    hidden_two_came = across(hidden_two_half, 2)
    mlp_half = tensor_sum(
        lambda rows: jnp.dot(rows, down_weight, preferred_element_type=float32), activated
    )
    grad_down = jnp.einsum("tf,td->fd", activated, out_cotangent, preferred_element_type=float32)
    grad_up = jnp.einsum("td,tcf->cfd", hidden_two, grad_up_parts, preferred_element_type=float32)
    gain_grad_two = jnp.einsum("cfd,cdf->d", grad_up, up_weight.astype(float32)) / gain_two
    hidden_two_came, mlp_half, _, _ = lax.optimization_barrier(
        (hidden_two_came, mlp_half, grad_up, grad_down)
    )
    grad_up, grad_down = lax.psum((grad_up, grad_down), "dp")
    grad_hidden_two = hidden_two_half + hidden_two_came
    mlp_came = across(mlp_half, 2)
    cot_mine = rows_of(out_cotangent, core, half_rows).astype(float32)
    cot_other = rows_of(out_cotangent, 1 - core, half_rows).astype(float32)
    norm_two_part = norm_two_pull(grad_hidden_two)[0]
    branch_mine = (cot_mine + norm_two_part).astype(bfloat)
    branch_other = (cot_other + across(norm_two_part, 1)).astype(bfloat)
    grad_branch = place_two(branch_mine, branch_other, core).reshape(token_rows, width)

    grad_out = jnp.einsum("te,td->ed", attended, grad_branch, preferred_element_type=float32)
    grad_attended = jnp.einsum("td,ed->te", grad_branch, out_weight, preferred_element_type=float32)
    grad_attended = grad_attended.reshape(blocks, block, heads_local, HD).astype(bfloat)
    probs_again = jnp.exp(masked_scores(query_blocks, key_window, allowed) - log_total)
    grad_value_window = jnp.einsum(
        "nhqk,nqhd->nkhd", probs_again.astype(bfloat), grad_attended, preferred_element_type=float32
    )
    grad_probs = jnp.einsum(
        "nqhd,nkhd->nhqk", grad_attended, value_window, preferred_element_type=float32
    )
    grad_scores = probs_again * (
        grad_probs - jnp.sum(probs_again * grad_probs, axis=-1, keepdims=True)
    )
    grad_scores = grad_scores.astype(bfloat)
    grad_query = jnp.einsum(
        "nhqk,nkhd->nqhd", grad_scores, key_window, preferred_element_type=float32
    ) * HD ** (-0.5)
    grad_key_window = jnp.einsum(
        "nhqk,nqhd->nkhd", grad_scores, query_blocks, preferred_element_type=float32
    ) * HD ** (-0.5)
    grad_query = grad_query.reshape(token_rows, heads_local, HD)
    grad_keys = fold_window(grad_key_window, block)
    grad_values = fold_window(grad_value_window, block)
    grad_query_proj = query_pull(grad_query)[0]
    grad_key_proj = key_pull(grad_keys)[0]
    grad_value_proj = grad_values.reshape(token_rows, -1)
    grad_projected = jnp.stack([grad_query_proj, grad_key_proj, grad_value_proj], axis=1).astype(
        bfloat
    )
    mlp_came, grad_projected = lax.optimization_barrier((mlp_came, grad_projected))
    both_branches = attn_branch + (mlp_half + mlp_came)
    out_mine = (layer_mine + both_branches).astype(bfloat)
    out_other = (layer_other + across(both_branches, 1)).astype(bfloat)
    layer_out = place_two(out_mine, out_other, core).reshape(token_rows, width)

    hidden_one_half = tensor_sum(
        lambda rows: jnp.einsum("tce,cde->td", rows, qkv_weight, preferred_element_type=float32),
        grad_projected,
    )
    grad_qkv = jnp.einsum(
        "td,tce->ced", hidden_one, grad_projected, preferred_element_type=float32
    )
    gain_grad_one = jnp.einsum("ced,cde->d", grad_qkv, qkv_weight.astype(float32)) / gain_one
    hidden_one_came = across(hidden_one_half, 2)
    gains = jnp.stack([gain_grad_one, gain_grad_two] + [jnp.zeros((width,), float32)] * 6)
    late = [grad_qkv.reshape(3 * columns, width), grad_out]
    late_rows = 3 * columns + grad_out.shape[0]
    unit = 16 * dp_size
    padded = -(-late_rows // unit) * unit
    if padded > late_rows:
        late.append(jnp.zeros((padded - late_rows, width), float32))
    late, gains = late_sum(jnp.concatenate(late, axis=0), gains, dp_size)
    grad_hidden_one = hidden_one_half + hidden_one_came
    norm_one_pull = jax.vjp(lambda rows: layer_norm(rows, gain_one), layer_mine)[1]
    both_norms = norm_two_part + norm_one_pull(grad_hidden_one)[0]
    input_mine = (cot_mine + both_norms).astype(bfloat)
    input_other = (cot_other + across(both_norms, 1)).astype(bfloat)
    input_grad = place_two(input_mine, input_other, core).reshape(token_rows, width)

    grad_qkv = late[: 3 * columns].reshape(3, columns, width)
    grad_out = late[3 * columns : late_rows]
    grad_up = grad_up.transpose(0, 2, 1)
    grad_qkv = grad_qkv.transpose(0, 2, 1)
    return (layer_out, input_grad, grad_qkv, grad_out, grad_up, grad_down, gains[0], gains[1])


def solution(mesh):
    return jax.shard_map(
        functools.partial(per_device, mesh.shape["tensor"], mesh.shape["dp"]),
        mesh=mesh,
        in_specs=(
            P("dp", None),
            P("dp"),
            P(None, None, "tensor"),
            P("tensor", None),
            P(None, None, "tensor"),
            P("tensor", None),
            P(),
            P(),
            P("dp", None),
        ),
        out_specs=(
            P("dp", None),
            P("dp", None),
            P(None, None, "tensor"),
            P("tensor", None),
            P(None, None, "tensor"),
            P("tensor", None),
            P(),
            P(),
        ),
        check_vma=False,
    )
```

```python
import functools

import jax
import jax.numpy as jnp
from jax import lax
from jax.experimental import pallas as pl
from jax.experimental.pallas import tpu as pltpu
from jax.sharding import PartitionSpec as P

HD = 64
HALF = 64


def layer_norm(values, gain):
    row_mean = jnp.mean(values, axis=-1, keepdims=True)
    centred = values - row_mean
    variance = jnp.mean(centred * centred, axis=-1, keepdims=True)
    return centred * lax.rsqrt(variance + 1e-05) * gain


def exact_gelu(values):
    return jax.nn.gelu(values, approximate=False)


def tables(places):
    half_dim = HD // 2
    freqs = 10000.0 ** (-jnp.arange(half_dim, dtype=jnp.float32) * 2.0 / HD)
    angles = places.astype(jnp.float32)[:, None] * freqs[None, :]
    angles = jnp.concatenate([angles, angles], axis=-1)
    return (jnp.cos(angles), jnp.sin(angles))


def rotate(values, cosine_table, sine_table):
    half_dim = values.shape[-1] // 2
    turned = jnp.concatenate([-values[..., half_dim:], values[..., :half_dim]], axis=-1)
    return values * cosine_table[:, None, :] + turned * sine_table[:, None, :]


def window(array, block, fill):
    blocks = array.shape[0] // block
    widths = [(block, block)] + [(0, 0)] * (array.ndim - 1)
    padded = jnp.pad(array, widths, constant_values=fill)
    shaped = padded.reshape((blocks + 2, block) + array.shape[1:])
    return jnp.concatenate([shaped[:-2], shaped[1:-1], shaped[2:]], axis=1)


def fold_window(pieces, block):
    blocks = pieces.shape[0]
    rest = [(0, 0)] * (pieces.ndim - 1)
    middle_part = pieces[:, block : 2 * block]
    from_before = jnp.pad(pieces[:-1, 2 * block :], [(1, 0)] + rest)
    from_after = jnp.pad(pieces[1:, :block], [(0, 1)] + rest)
    whole = middle_part + from_before + from_after
    return whole.reshape((blocks * block,) + pieces.shape[2:])


def masked_scores(query_blocks, key_window, allowed):
    scores = jnp.einsum(
        "nqhd,nkhd->nhqk", query_blocks, key_window, preferred_element_type=jnp.float32
    ) * HD ** (-0.5)
    return jnp.where(allowed[:, None], scores, -1e30)


def swap(array, axis, mask, size):
    return lax.ppermute(array, axis, [(i, i ^ mask) for i in range(size)])


def halve(array):
    return array * 0.5


def rows_of(array, part, rows):
    return lax.dynamic_slice_in_dim(array, part * rows, rows, axis=0)


def place_two(mine, other, bit):
    both = jnp.zeros((2,) + mine.shape, mine.dtype)
    both = lax.dynamic_update_index_in_dim(both, mine, bit, 0)
    return lax.dynamic_update_index_in_dim(both, other, 1 - bit, 0)


def masks_of(size):
    masks = []
    mask = 1
    while mask < size:
        masks.append(mask)
        mask *= 2
    return masks


def chains_of(rows, dp_size):
    unit = 8 * dp_size
    units = rows // unit
    count = min(4, units)
    masks = masks_of(dp_size)
    chains = []
    start = 0
    for index in range(count):
        size = (units // count + (1 if index >= count - units % count else 0)) * unit
        order = masks[1:] + masks[:1] if index == 1 else masks
        chains.append((start, size, order))
        start += size
    return chains


def sum_kernel(dp_size, whole, gains, summed, gain_sum, kept, landed, gain_held, gain_landed, *sems):
    send_sem, recv_sem, back_send, back_recv, gain_send, gain_recv = sems
    me = lax.axis_index("dp")
    lane = lax.axis_index("tensor")
    masks = masks_of(dp_size)
    steps = len(masks)
    chains = chains_of(whole.shape[0], dp_size)
    orders = [order for _, _, order in chains]
    hops = [("tensor", 1), ("tensor", 2)] + [("dp", mask) for mask in masks]

    def flip(axis, mask):
        at = me if axis == "dp" else lane
        bit = (at // mask) % 2
        return {axis: at + mask * (1 - 2 * bit)}

    barrier = pltpu.get_barrier_semaphore()
    for axis, mask in hops:
        pl.semaphore_signal(
            barrier, inc=1, device_id=flip(axis, mask), device_id_type=pl.DeviceIdType.MESH
        )
    pl.semaphore_wait(barrier, len(hops))

    def span(start, size):
        return pl.ds(pl.multiple_of(start, 8), size)

    def gain_copy(step):
        return pltpu.make_async_remote_copy(
            src_ref=gain_held.at[step],
            dst_ref=gain_landed.at[step],
            send_sem=gain_send.at[step],
            recv_sem=gain_recv.at[step],
            device_id=flip(*hops[step]),
            device_id_type=pl.DeviceIdType.MESH,
        )

    def out_copy(chain, step, start, size):
        mask = orders[chain][step]
        bit = (me // mask) % 2
        base = chains[chain][0] + chains[chain][1] - 2 * size
        source = whole if step == 0 else kept
        return pltpu.make_async_remote_copy(
            src_ref=source.at[span(start + (1 - bit) * size, size)],
            dst_ref=landed.at[pl.ds(base, size)],
            send_sem=send_sem.at[chain, step],
            recv_sem=recv_sem.at[chain, step],
            device_id=flip("dp", mask),
            device_id_type=pl.DeviceIdType.MESH,
        )

    def back_copy(chain, step, start, size):
        return pltpu.make_async_remote_copy(
            src_ref=summed.at[span(start, size)],
            dst_ref=summed.at[span(start, size)],
            send_sem=back_send.at[chain, step],
            recv_sem=back_recv.at[chain, step],
            device_id=flip("dp", orders[chain][step]),
            device_id_type=pl.DeviceIdType.MESH,
        )

    starts = [start for start, _, _ in chains]
    sizes = [size // 2 for _, size, _ in chains]
    copies = [out_copy(chain, 0, starts[chain], sizes[chain]) for chain in range(len(chains))]
    for copy in copies:
        copy.start()
    gain_held[0] = gains[...]
    gain_step = 0
    small = gain_copy(0)
    small.start()

    def advance_gains(small, step):
        small.wait()
        gain_held[step + 1] = gain_held[step] + gain_landed[step]
        if step + 1 < len(hops):
            small = gain_copy(step + 1)
            small.start()
        return small

    for step in range(steps):
        for chain in range(len(chains)):
            size = sizes[chain]
            mask = orders[chain][step]
            bit = (me // mask) % 2
            copies[chain].wait()
            mine = span(starts[chain] + bit * size, size)
            base = chains[chain][0] + chains[chain][1] - 2 * size
            source = whole if step == 0 else kept
            total = source[mine, :] + landed[pl.ds(base, size), :]
            starts[chain] = starts[chain] + bit * size
            if step + 1 < steps:
                kept[mine, :] = total
                copies[chain] = out_copy(chain, step + 1, starts[chain], size // 2)
            else:
                summed[mine, :] = total
                copies[chain] = back_copy(chain, step, starts[chain], size)
            copies[chain].start()
            if step + 1 < steps:
                sizes[chain] = size // 2
        if gain_step < len(hops):
            small = advance_gains(small, gain_step)
            gain_step += 1
    for step in reversed(range(steps)):
        for chain in range(len(chains)):
            size = sizes[chain]
            copies[chain].wait()
            bit = (me // orders[chain][step]) % 2
            starts[chain] = starts[chain] - bit * size
            if step > 0:
                copies[chain] = back_copy(chain, step - 1, starts[chain], 2 * size)
                copies[chain].start()
            sizes[chain] = size * 2
        if gain_step < len(hops):
            small = advance_gains(small, gain_step)
            gain_step += 1
    gain_sum[...] = gain_held[len(hops)]


def dp_sum(pieces, gain, dp_size, collective_id):
    width = gain.shape[0]
    rows = sum(piece.shape[0] for piece in pieces)
    unit = 8 * dp_size
    padded = -(-rows // unit) * unit
    if padded > rows:
        pieces = pieces + [jnp.zeros((padded - rows, width), jnp.float32)]
    whole = jnp.concatenate(pieces, axis=0)
    gains = jnp.concatenate([gain[None], jnp.zeros((7, width), jnp.float32)], axis=0)
    steps = len(masks_of(dp_size))
    count = len(chains_of(padded, dp_size))
    hops = steps + 2
    vmem = pl.BlockSpec(memory_space=pltpu.VMEM)
    summed, gains = pl.pallas_call(
        functools.partial(sum_kernel, dp_size),
        out_shape=(
            jax.ShapeDtypeStruct(whole.shape, jnp.float32),
            jax.ShapeDtypeStruct(gains.shape, jnp.float32),
        ),
        in_specs=[vmem, vmem],
        out_specs=(vmem, vmem),
        scratch_shapes=[
            pltpu.VMEM(whole.shape, jnp.float32),
            pltpu.VMEM(whole.shape, jnp.float32),
            pltpu.VMEM((hops + 1,) + gains.shape, jnp.float32),
            pltpu.VMEM((hops,) + gains.shape, jnp.float32),
        ]
        + [pltpu.SemaphoreType.DMA((count, steps))] * 4
        + [pltpu.SemaphoreType.DMA((hops,))] * 2,
        compiler_params=pltpu.CompilerParams(
            collective_id=collective_id, has_side_effects=True, vmem_limit_bytes=32 * 1024 * 1024
        ),
        cost_estimate=pl.CostEstimate(flops=0, bytes_accessed=200000000, transcendentals=0),
    )(whole, gains)
    return summed[:rows], gains[0]


def per_device(
    tensor_size,
    dp_size,
    layer_in,
    doc_ids,
    qkv_weight,
    out_weight,
    up_weight,
    down_weight,
    norm1_gain,
    norm2_gain,
    out_cotangent,
):
    token_rows, width = layer_in.shape
    heads_local = qkv_weight.shape[2] // HD
    columns = heads_local * HD
    block = 2 * HALF
    blocks = token_rows // block
    half_rows = token_rows // 2
    lane = lax.axis_index("tensor")
    me = lax.axis_index("dp")
    core = lane % 2
    bfloat = jnp.bfloat16
    float32 = jnp.float32

    def across(array, mask):
        return swap(array, "tensor", mask, tensor_size)

    weight_float = out_weight.astype(float32) * 2.0
    weight_two = across(weight_float, 2)
    weight_one = across(weight_float, 1)
    weight_three = across(weight_two, 1)
    out_full = jnp.zeros((tensor_size,) + out_weight.shape, bfloat)
    out_full = lax.dynamic_update_index_in_dim(out_full, out_weight, lane, 0)
    for mask, piece in ((1, weight_one), (2, weight_two), (3, weight_three)):
        out_full = lax.dynamic_update_index_in_dim(
            out_full, halve(piece).astype(bfloat), lane ^ mask, 0
        )

    slot_index = jnp.arange(token_rows, dtype=jnp.int32)
    previous = jnp.concatenate([doc_ids[:1] - 1, doc_ids[:-1]])
    starts = jnp.where(doc_ids != previous, slot_index, 0)
    places = slot_index - lax.cummax(starts, axis=0)
    cosine_table, sine_table = tables(places)
    query_slots = slot_index.reshape(blocks, block)
    key_slots = (
        jnp.arange(blocks, dtype=jnp.int32)[:, None] * block
        - block
        + jnp.arange(3 * block, dtype=jnp.int32)[None, :]
    )
    query_docs = doc_ids.reshape(blocks, block)
    key_docs = window(doc_ids, block, -2)
    distance = jnp.abs(query_slots[:, :, None] - key_slots[:, None, :])
    same_doc = (query_docs[:, :, None] == key_docs[:, None, :]) & (query_docs[:, :, None] >= 0)
    allowed = same_doc & (distance <= HALF) | (distance == 0)

    def turn(values):
        return rotate(values.reshape(token_rows, heads_local, HD), cosine_table, sine_table)

    gain_one = norm1_gain.astype(float32)
    gain_two = norm2_gain.astype(float32)
    layer_float = layer_in.astype(float32)
    hidden_one = layer_norm(layer_float, gain_one).astype(bfloat)
    projected = jnp.einsum("td,cde->cte", hidden_one, qkv_weight, preferred_element_type=float32)
    query_float, query_pull = jax.vjp(turn, projected[0])
    key_float, key_pull = jax.vjp(turn, projected[1])
    query = query_float.astype(bfloat)
    keys_rot = key_float.astype(bfloat)
    values = projected[2].reshape(token_rows, heads_local, HD).astype(bfloat)
    query_blocks = query.reshape(blocks, block, heads_local, HD)
    key_window = window(keys_rot, block, 0)
    value_window = window(values, block, 0)
    scores = masked_scores(query_blocks, key_window, allowed)
    top_score = jnp.max(scores, axis=-1, keepdims=True)
    expo = jnp.exp(scores - top_score)
    total = jnp.sum(expo, axis=-1, keepdims=True)
    probs = expo / total
    log_total = top_score + jnp.log(total)
    attended = jnp.einsum(
        "nhqk,nkhd->nqhd", probs.astype(bfloat), value_window, preferred_element_type=float32
    )
    attended_float = attended.reshape(token_rows, columns)
    attended = attended_float.astype(bfloat)

    attended_mine = rows_of(attended, core, half_rows)
    doubled = attended_float * 2.0
    float_mine = rows_of(doubled, core, half_rows)
    float_other = rows_of(doubled, 1 - core, half_rows)
    from_three = across(float_other, 3)
    from_two = across(float_mine, 2)
    from_one = across(float_other, 1)
    all_heads = jnp.zeros((tensor_size, half_rows, columns), bfloat)
    all_heads = lax.dynamic_update_index_in_dim(all_heads, attended_mine, lane, 0)
    for mask, piece in ((1, from_one), (2, from_two), (3, from_three)):
        all_heads = lax.dynamic_update_index_in_dim(
            all_heads, halve(piece).astype(bfloat), lane ^ mask, 0
        )
    attn_branch = jnp.einsum("jte,jed->td", all_heads, out_full, preferred_element_type=float32)
    layer_mine = rows_of(layer_float, core, half_rows)
    layer_other = rows_of(layer_float, 1 - core, half_rows)
    middle = layer_mine + attn_branch
    norm_two_pull = jax.vjp(lambda rows: layer_norm(rows, gain_two), middle)[1]
    normed_two = layer_norm(middle, 1.0)
    hidden_mine = (normed_two * gain_two).astype(bfloat)
    hidden_other = (across(normed_two, 1) * gain_two).astype(bfloat)
    hidden_two = place_two(hidden_mine, hidden_other, core).reshape(token_rows, width)

    up_parts = jnp.einsum("td,cdf->ctf", hidden_two, up_weight, preferred_element_type=float32)
    gate_in = up_parts[0]
    gate_up = up_parts[1]
    gelu_value, gelu_pull = jax.vjp(exact_gelu, gate_in)
    activated = (gelu_value * gate_up).astype(bfloat)
    grad_act = jnp.einsum("td,fd->tf", out_cotangent, down_weight, preferred_element_type=float32)
    grad_gate_in = gelu_pull(grad_act * gate_up)[0]
    grad_gate_up = grad_act * gelu_value
    grad_up_parts = jnp.stack([grad_gate_in, grad_gate_up], axis=1).astype(bfloat)

    def tensor_sum(product, rows_in):
        part_other = product(rows_of(rows_in, 1 - core, half_rows))
        arrived = across(part_other, 1)
        part_mine = product(rows_of(rows_in, core, half_rows))
        return part_mine + arrived

    hidden_two_half = tensor_sum(
        lambda rows: jnp.einsum("tcf,cdf->td", rows, up_weight, preferred_element_type=float32),
        grad_up_parts,
    )
    hidden_two_came = across(hidden_two_half, 2)
    activated_after, _ = lax.optimization_barrier((activated, hidden_two_half))
    mlp_half = tensor_sum(
        lambda rows: jnp.dot(rows, down_weight, preferred_element_type=float32), activated_after
    )
    mlp_came = across(mlp_half, 2)
    grad_down = jnp.einsum("tf,td->fd", activated, out_cotangent, preferred_element_type=float32)
    grad_up = jnp.einsum("td,tcf->cfd", hidden_two, grad_up_parts, preferred_element_type=float32)
    units = grad_down.shape[0]
    gain_grad_two = jnp.einsum("cfd,cdf->d", grad_up, up_weight.astype(float32)) / gain_two
    grad_up, grad_down, gain_grad_two, mlp_half = lax.optimization_barrier(
        (grad_up, grad_down, gain_grad_two, mlp_half)
    )
    early, gain_grad_two = dp_sum(
        [grad_up.reshape(2 * units, width), grad_down], gain_grad_two, dp_size, 1
    )
    hidden_two_came, mlp_came, early = lax.optimization_barrier((hidden_two_came, mlp_came, early))
    grad_up = early[: 2 * units].reshape(2, units, width).transpose(0, 2, 1)
    grad_down = early[2 * units :]
    grad_hidden_two = hidden_two_half + hidden_two_came
    cot_mine = rows_of(out_cotangent, core, half_rows).astype(float32)
    cot_other = rows_of(out_cotangent, 1 - core, half_rows).astype(float32)
    norm_two_part = norm_two_pull(grad_hidden_two)[0]
    branch_mine = (cot_mine + norm_two_part).astype(bfloat)
    branch_other = (cot_other + across(norm_two_part, 1)).astype(bfloat)
    grad_branch = place_two(branch_mine, branch_other, core).reshape(token_rows, width)

    grad_out = jnp.einsum("te,td->ed", attended, grad_branch, preferred_element_type=float32)
    grad_attended = jnp.einsum("td,ed->te", grad_branch, out_weight, preferred_element_type=float32)
    grad_attended = grad_attended.reshape(blocks, block, heads_local, HD).astype(bfloat)
    probs_again = jnp.exp(masked_scores(query_blocks, key_window, allowed) - log_total)
    grad_value_window = jnp.einsum(
        "nhqk,nqhd->nkhd", probs_again.astype(bfloat), grad_attended, preferred_element_type=float32
    )
    grad_probs = jnp.einsum(
        "nqhd,nkhd->nhqk", grad_attended, value_window, preferred_element_type=float32
    )
    grad_scores = probs_again * (
        grad_probs - jnp.sum(probs_again * grad_probs, axis=-1, keepdims=True)
    )
    grad_scores = grad_scores.astype(bfloat)
    grad_query = jnp.einsum(
        "nhqk,nkhd->nqhd", grad_scores, key_window, preferred_element_type=float32
    ) * HD ** (-0.5)
    grad_key_window = jnp.einsum(
        "nhqk,nqhd->nkhd", grad_scores, query_blocks, preferred_element_type=float32
    ) * HD ** (-0.5)
    grad_query = grad_query.reshape(token_rows, heads_local, HD)
    grad_keys = fold_window(grad_key_window, block)
    grad_values = fold_window(grad_value_window, block)
    grad_query_proj = query_pull(grad_query)[0]
    grad_key_proj = key_pull(grad_keys)[0]
    grad_value_proj = grad_values.reshape(token_rows, -1)
    grad_projected = jnp.stack([grad_query_proj, grad_key_proj, grad_value_proj], axis=1).astype(
        bfloat
    )
    both_branches = attn_branch + (mlp_half + mlp_came)
    out_mine = (layer_mine + both_branches).astype(bfloat)
    out_other = (layer_other + across(both_branches, 1)).astype(bfloat)
    layer_out = place_two(out_mine, out_other, core).reshape(token_rows, width)

    hidden_one_half = tensor_sum(
        lambda rows: jnp.einsum("tce,cde->td", rows, qkv_weight, preferred_element_type=float32),
        grad_projected,
    )
    grad_qkv = jnp.einsum(
        "td,tce->ced", hidden_one, grad_projected, preferred_element_type=float32
    )
    gain_grad_one = jnp.einsum("ced,cde->d", grad_qkv, qkv_weight.astype(float32)) / gain_one
    hidden_one_came = across(hidden_one_half, 2)
    late, gain_grad_one = dp_sum(
        [grad_qkv.reshape(3 * columns, width), grad_out], gain_grad_one, dp_size, 0
    )
    hidden_one_came, late = lax.optimization_barrier((hidden_one_came, late))
    grad_hidden_one = hidden_one_half + hidden_one_came
    norm_one_pull = jax.vjp(lambda rows: layer_norm(rows, gain_one), layer_mine)[1]
    both_norms = norm_two_part + norm_one_pull(grad_hidden_one)[0]
    input_mine = (cot_mine + both_norms).astype(bfloat)
    input_other = (cot_other + across(both_norms, 1)).astype(bfloat)
    input_grad = place_two(input_mine, input_other, core).reshape(token_rows, width)

    grad_qkv = late[: 3 * columns].reshape(3, columns, width)
    grad_out = late[3 * columns :]
    grad_qkv = grad_qkv.transpose(0, 2, 1)
    return (layer_out, input_grad, grad_qkv, grad_out, grad_up, grad_down, gain_grad_one, gain_grad_two)


def solution(mesh):
    return jax.shard_map(
        functools.partial(per_device, mesh.shape["tensor"], mesh.shape["dp"]),
        mesh=mesh,
        in_specs=(
            P("dp", None),
            P("dp"),
            P(None, None, "tensor"),
            P("tensor", None),
            P(None, None, "tensor"),
            P("tensor", None),
            P(),
            P(),
            P("dp", None),
        ),
        out_specs=(
            P("dp", None),
            P("dp", None),
            P(None, None, "tensor"),
            P("tensor", None),
            P(None, None, "tensor"),
            P("tensor", None),
            P(),
            P(),
        ),
        check_vma=False,
    )
```

```python
import functools

import jax
import jax.numpy as jnp
from jax import lax
from jax.experimental import pallas as pl
from jax.experimental.pallas import tpu as pltpu
from jax.sharding import PartitionSpec as P

HD = 64
HALF = 64


def layer_norm(values, gain):
    row_mean = jnp.mean(values, axis=-1, keepdims=True)
    centred = values - row_mean
    variance = jnp.mean(centred * centred, axis=-1, keepdims=True)
    return centred * lax.rsqrt(variance + 1e-05) * gain


def exact_gelu(values):
    return jax.nn.gelu(values, approximate=False)


def tables(places):
    half_dim = HD // 2
    freqs = 10000.0 ** (-jnp.arange(half_dim, dtype=jnp.float32) * 2.0 / HD)
    angles = places.astype(jnp.float32)[:, None] * freqs[None, :]
    angles = jnp.concatenate([angles, angles], axis=-1)
    return (jnp.cos(angles), jnp.sin(angles))


def rotate(values, cosine_table, sine_table):
    half_dim = values.shape[-1] // 2
    turned = jnp.concatenate([-values[..., half_dim:], values[..., :half_dim]], axis=-1)
    return values * cosine_table[:, None, :] + turned * sine_table[:, None, :]


def window(array, block, fill):
    blocks = array.shape[0] // block
    widths = [(block, block)] + [(0, 0)] * (array.ndim - 1)
    padded = jnp.pad(array, widths, constant_values=fill)
    shaped = padded.reshape((blocks + 2, block) + array.shape[1:])
    return jnp.concatenate([shaped[:-2], shaped[1:-1], shaped[2:]], axis=1)


def fold_window(pieces, block):
    blocks = pieces.shape[0]
    rest = [(0, 0)] * (pieces.ndim - 1)
    middle_part = pieces[:, block : 2 * block]
    from_before = jnp.pad(pieces[:-1, 2 * block :], [(1, 0)] + rest)
    from_after = jnp.pad(pieces[1:, :block], [(0, 1)] + rest)
    whole = middle_part + from_before + from_after
    return whole.reshape((blocks * block,) + pieces.shape[2:])


def masked_scores(query_blocks, key_window, allowed):
    scores = jnp.einsum(
        "nqhd,nkhd->nhqk", query_blocks, key_window, preferred_element_type=jnp.float32
    ) * HD ** (-0.5)
    return jnp.where(allowed[:, None], scores, -1e30)


def swap(array, axis, mask, size):
    return lax.ppermute(array, axis, [(i, i ^ mask) for i in range(size)])


def halve(array):
    return array * 0.5


def rows_of(array, part, rows):
    return lax.dynamic_slice_in_dim(array, part * rows, rows, axis=0)


def place_two(mine, other, bit):
    both = jnp.zeros((2,) + mine.shape, mine.dtype)
    both = lax.dynamic_update_index_in_dim(both, mine, bit, 0)
    return lax.dynamic_update_index_in_dim(both, other, 1 - bit, 0)


def masks_of(size):
    masks = []
    mask = 1
    while mask < size:
        masks.append(mask)
        mask *= 2
    return masks


def chains_of(rows, dp_size):
    unit = 8 * dp_size
    units = rows // unit
    count = min(6, units)
    masks = masks_of(dp_size)
    chains = []
    start = 0
    for index in range(count):
        size = (units // count + (1 if index >= count - units % count else 0)) * unit
        order = masks[1:2] + masks[:1] + masks[2:] if index % 2 else masks
        chains.append((start, size, order))
        start += size
    return chains


def sum_kernel(dp_size, whole, gains, summed, gain_sum, kept, landed, gain_held, gain_landed, *sems):
    send_sem, recv_sem, back_send, back_recv, gain_send, gain_recv = sems
    me = lax.axis_index("dp")
    lane = lax.axis_index("tensor")
    masks = masks_of(dp_size)
    steps = len(masks)
    chains = chains_of(whole.shape[0], dp_size)
    orders = [order for _, _, order in chains]
    hops = [("tensor", 1), ("tensor", 2)] + [("dp", mask) for mask in masks]

    def flip(axis, mask):
        at = me if axis == "dp" else lane
        bit = (at // mask) % 2
        return {axis: at + mask * (1 - 2 * bit)}

    barrier = pltpu.get_barrier_semaphore()
    for axis, mask in hops:
        pl.semaphore_signal(
            barrier, inc=1, device_id=flip(axis, mask), device_id_type=pl.DeviceIdType.MESH
        )
    pl.semaphore_wait(barrier, len(hops))

    def span(start, size):
        return pl.ds(pl.multiple_of(start, 8), size)

    def gain_copy(step):
        return pltpu.make_async_remote_copy(
            src_ref=gain_held.at[step],
            dst_ref=gain_landed.at[step],
            send_sem=gain_send.at[step],
            recv_sem=gain_recv.at[step],
            device_id=flip(*hops[step]),
            device_id_type=pl.DeviceIdType.MESH,
        )

    def out_copy(chain, step, start, size):
        mask = orders[chain][step]
        bit = (me // mask) % 2
        base = chains[chain][0] + chains[chain][1] - 2 * size
        source = whole if step == 0 else kept
        return pltpu.make_async_remote_copy(
            src_ref=source.at[span(start + (1 - bit) * size, size)],
            dst_ref=landed.at[pl.ds(base, size)],
            send_sem=send_sem.at[chain, step],
            recv_sem=recv_sem.at[chain, step],
            device_id=flip("dp", mask),
            device_id_type=pl.DeviceIdType.MESH,
        )

    def back_copy(chain, step, start, size):
        return pltpu.make_async_remote_copy(
            src_ref=summed.at[span(start, size)],
            dst_ref=summed.at[span(start, size)],
            send_sem=back_send.at[chain, step],
            recv_sem=back_recv.at[chain, step],
            device_id=flip("dp", orders[chain][step]),
            device_id_type=pl.DeviceIdType.MESH,
        )

    starts = [start for start, _, _ in chains]
    sizes = [size // 2 for _, size, _ in chains]
    copies = [out_copy(chain, 0, starts[chain], sizes[chain]) for chain in range(len(chains))]
    for copy in copies:
        copy.start()
    gain_held[0] = gains[...]
    gain_step = 0
    small = gain_copy(0)
    small.start()

    def advance_gains(small, step):
        small.wait()
        gain_held[step + 1] = gain_held[step] + gain_landed[step]
        if step + 1 < len(hops):
            small = gain_copy(step + 1)
            small.start()
        return small

    for step in range(steps):
        for chain in range(len(chains)):
            size = sizes[chain]
            mask = orders[chain][step]
            bit = (me // mask) % 2
            copies[chain].wait()
            mine = span(starts[chain] + bit * size, size)
            base = chains[chain][0] + chains[chain][1] - 2 * size
            source = whole if step == 0 else kept
            total = source[mine, :] + landed[pl.ds(base, size), :]
            starts[chain] = starts[chain] + bit * size
            if step + 1 < steps:
                kept[mine, :] = total
                copies[chain] = out_copy(chain, step + 1, starts[chain], size // 2)
            else:
                summed[mine, :] = total
                copies[chain] = back_copy(chain, step, starts[chain], size)
            copies[chain].start()
            if step + 1 < steps:
                sizes[chain] = size // 2
        if gain_step < len(hops):
            small = advance_gains(small, gain_step)
            gain_step += 1
    for step in reversed(range(steps)):
        for chain in range(len(chains)):
            size = sizes[chain]
            copies[chain].wait()
            bit = (me // orders[chain][step]) % 2
            starts[chain] = starts[chain] - bit * size
            if step > 0:
                copies[chain] = back_copy(chain, step - 1, starts[chain], 2 * size)
                copies[chain].start()
            sizes[chain] = size * 2
        if gain_step < len(hops):
            small = advance_gains(small, gain_step)
            gain_step += 1
    gain_sum[...] = gain_held[len(hops)]


def dp_sum(pieces, gain, dp_size, collective_id):
    width = gain.shape[0]
    rows = sum(piece.shape[0] for piece in pieces)
    unit = 8 * dp_size
    padded = -(-rows // unit) * unit
    if padded > rows:
        pieces = pieces + [jnp.zeros((padded - rows, width), jnp.float32)]
    whole = jnp.concatenate(pieces, axis=0)
    gains = jnp.concatenate([gain[None], jnp.zeros((7, width), jnp.float32)], axis=0)
    steps = len(masks_of(dp_size))
    count = len(chains_of(padded, dp_size))
    hops = steps + 2
    vmem = pl.BlockSpec(memory_space=pltpu.VMEM)
    summed, gains = pl.pallas_call(
        functools.partial(sum_kernel, dp_size),
        out_shape=(
            jax.ShapeDtypeStruct(whole.shape, jnp.float32),
            jax.ShapeDtypeStruct(gains.shape, jnp.float32),
        ),
        in_specs=[vmem, vmem],
        out_specs=(vmem, vmem),
        scratch_shapes=[
            pltpu.VMEM(whole.shape, jnp.float32),
            pltpu.VMEM(whole.shape, jnp.float32),
            pltpu.VMEM((hops + 1,) + gains.shape, jnp.float32),
            pltpu.VMEM((hops,) + gains.shape, jnp.float32),
        ]
        + [pltpu.SemaphoreType.DMA((count, steps))] * 4
        + [pltpu.SemaphoreType.DMA((hops,))] * 2,
        compiler_params=pltpu.CompilerParams(
            collective_id=collective_id, has_side_effects=True, vmem_limit_bytes=32 * 1024 * 1024
        ),
        cost_estimate=pl.CostEstimate(flops=0, bytes_accessed=200000000, transcendentals=0),
    )(whole, gains)
    return summed[:rows], gains[0]


def per_device(
    tensor_size,
    dp_size,
    layer_in,
    doc_ids,
    qkv_weight,
    out_weight,
    up_weight,
    down_weight,
    norm1_gain,
    norm2_gain,
    out_cotangent,
):
    token_rows, width = layer_in.shape
    heads_local = qkv_weight.shape[2] // HD
    columns = heads_local * HD
    block = 2 * HALF
    blocks = token_rows // block
    half_rows = token_rows // 2
    lane = lax.axis_index("tensor")
    me = lax.axis_index("dp")
    core = lane % 2
    bfloat = jnp.bfloat16
    float32 = jnp.float32

    def across(array, mask):
        return swap(array, "tensor", mask, tensor_size)

    weight_float = out_weight.astype(float32) * 2.0
    weight_two = across(weight_float, 2)
    weight_one = across(weight_float, 1)
    weight_three = across(weight_two, 1)
    out_full = jnp.zeros((tensor_size,) + out_weight.shape, bfloat)
    out_full = lax.dynamic_update_index_in_dim(out_full, out_weight, lane, 0)
    for mask, piece in ((1, weight_one), (2, weight_two), (3, weight_three)):
        out_full = lax.dynamic_update_index_in_dim(
            out_full, halve(piece).astype(bfloat), lane ^ mask, 0
        )

    slot_index = jnp.arange(token_rows, dtype=jnp.int32)
    previous = jnp.concatenate([doc_ids[:1] - 1, doc_ids[:-1]])
    starts = jnp.where(doc_ids != previous, slot_index, 0)
    places = slot_index - lax.cummax(starts, axis=0)
    cosine_table, sine_table = tables(places)
    query_slots = slot_index.reshape(blocks, block)
    key_slots = (
        jnp.arange(blocks, dtype=jnp.int32)[:, None] * block
        - block
        + jnp.arange(3 * block, dtype=jnp.int32)[None, :]
    )
    query_docs = doc_ids.reshape(blocks, block)
    key_docs = window(doc_ids, block, -2)
    distance = jnp.abs(query_slots[:, :, None] - key_slots[:, None, :])
    same_doc = (query_docs[:, :, None] == key_docs[:, None, :]) & (query_docs[:, :, None] >= 0)
    allowed = same_doc & (distance <= HALF) | (distance == 0)

    def turn(values):
        return rotate(values.reshape(token_rows, heads_local, HD), cosine_table, sine_table)

    gain_one = norm1_gain.astype(float32)
    gain_two = norm2_gain.astype(float32)
    layer_float = layer_in.astype(float32)
    hidden_one = layer_norm(layer_float, gain_one).astype(bfloat)
    projected = jnp.einsum("td,cde->cte", hidden_one, qkv_weight, preferred_element_type=float32)
    query_float, query_pull = jax.vjp(turn, projected[0])
    key_float, key_pull = jax.vjp(turn, projected[1])
    query = query_float.astype(bfloat)
    keys_rot = key_float.astype(bfloat)
    values = projected[2].reshape(token_rows, heads_local, HD).astype(bfloat)
    query_blocks = query.reshape(blocks, block, heads_local, HD)
    key_window = window(keys_rot, block, 0)
    value_window = window(values, block, 0)
    scores = masked_scores(query_blocks, key_window, allowed)
    top_score = jnp.max(scores, axis=-1, keepdims=True)
    expo = jnp.exp(scores - top_score)
    total = jnp.sum(expo, axis=-1, keepdims=True)
    probs = expo / total
    log_total = top_score + jnp.log(total)
    attended = jnp.einsum(
        "nhqk,nkhd->nqhd", probs.astype(bfloat), value_window, preferred_element_type=float32
    )
    attended_float = attended.reshape(token_rows, columns)
    attended = attended_float.astype(bfloat)

    attended_mine = rows_of(attended, core, half_rows)
    doubled = attended_float * 2.0
    float_mine = rows_of(doubled, core, half_rows)
    float_other = rows_of(doubled, 1 - core, half_rows)
    from_three = across(float_other, 3)
    from_two = across(float_mine, 2)
    from_one = across(float_other, 1)
    all_heads = jnp.zeros((tensor_size, half_rows, columns), bfloat)
    all_heads = lax.dynamic_update_index_in_dim(all_heads, attended_mine, lane, 0)
    for mask, piece in ((1, from_one), (2, from_two), (3, from_three)):
        all_heads = lax.dynamic_update_index_in_dim(
            all_heads, halve(piece).astype(bfloat), lane ^ mask, 0
        )
    attn_branch = jnp.einsum("jte,jed->td", all_heads, out_full, preferred_element_type=float32)
    layer_mine = rows_of(layer_float, core, half_rows)
    layer_other = rows_of(layer_float, 1 - core, half_rows)
    middle = layer_mine + attn_branch
    norm_two_pull = jax.vjp(lambda rows: layer_norm(rows, gain_two), middle)[1]
    normed_two = layer_norm(middle, 1.0)
    hidden_mine = (normed_two * gain_two).astype(bfloat)
    hidden_other = (across(normed_two, 1) * gain_two).astype(bfloat)
    hidden_two = place_two(hidden_mine, hidden_other, core).reshape(token_rows, width)

    up_parts = jnp.einsum("td,cdf->ctf", hidden_two, up_weight, preferred_element_type=float32)
    gate_in = up_parts[0]
    gate_up = up_parts[1]
    gelu_value, gelu_pull = jax.vjp(exact_gelu, gate_in)
    activated = (gelu_value * gate_up).astype(bfloat)
    grad_act = jnp.einsum("td,fd->tf", out_cotangent, down_weight, preferred_element_type=float32)
    grad_gate_in = gelu_pull(grad_act * gate_up)[0]
    grad_gate_up = grad_act * gelu_value
    grad_up_parts = jnp.stack([grad_gate_in, grad_gate_up], axis=1).astype(bfloat)

    def tensor_sum(product, rows_in):
        part_other = product(rows_of(rows_in, 1 - core, half_rows))
        arrived = across(part_other, 1)
        part_mine = product(rows_of(rows_in, core, half_rows))
        return part_mine + arrived

    hidden_two_half = tensor_sum(
        lambda rows: jnp.einsum("tcf,cdf->td", rows, up_weight, preferred_element_type=float32),
        grad_up_parts,
    )
    hidden_two_came = across(hidden_two_half, 2)
    activated_after, _ = lax.optimization_barrier((activated, hidden_two_half))
    mlp_half = tensor_sum(
        lambda rows: jnp.dot(rows, down_weight, preferred_element_type=float32), activated_after
    )
    mlp_came = across(mlp_half, 2)
    grad_down = jnp.einsum("tf,td->fd", activated, out_cotangent, preferred_element_type=float32)
    grad_up = jnp.einsum("td,tcf->cfd", hidden_two, grad_up_parts, preferred_element_type=float32)
    units = grad_down.shape[0]
    gain_grad_two = jnp.einsum("cfd,cdf->d", grad_up, up_weight.astype(float32)) / gain_two
    grad_up, grad_down, gain_grad_two, mlp_half = lax.optimization_barrier(
        (grad_up, grad_down, gain_grad_two, mlp_half)
    )
    early, gain_grad_two = dp_sum(
        [grad_up.reshape(2 * units, width), grad_down], gain_grad_two, dp_size, 1
    )
    hidden_two_came, mlp_came, early = lax.optimization_barrier((hidden_two_came, mlp_came, early))
    grad_up = early[: 2 * units].reshape(2, units, width).transpose(0, 2, 1)
    grad_down = early[2 * units :]
    grad_hidden_two = hidden_two_half + hidden_two_came
    cot_mine = rows_of(out_cotangent, core, half_rows).astype(float32)
    cot_other = rows_of(out_cotangent, 1 - core, half_rows).astype(float32)
    norm_two_part = norm_two_pull(grad_hidden_two)[0]
    branch_mine = (cot_mine + norm_two_part).astype(bfloat)
    branch_other = (cot_other + across(norm_two_part, 1)).astype(bfloat)
    grad_branch = place_two(branch_mine, branch_other, core).reshape(token_rows, width)

    grad_out = jnp.einsum("te,td->ed", attended, grad_branch, preferred_element_type=float32)
    grad_attended = jnp.einsum("td,ed->te", grad_branch, out_weight, preferred_element_type=float32)
    grad_attended = grad_attended.reshape(blocks, block, heads_local, HD).astype(bfloat)
    probs_again = jnp.exp(masked_scores(query_blocks, key_window, allowed) - log_total)
    grad_value_window = jnp.einsum(
        "nhqk,nqhd->nkhd", probs_again.astype(bfloat), grad_attended, preferred_element_type=float32
    )
    grad_probs = jnp.einsum(
        "nqhd,nkhd->nhqk", grad_attended, value_window, preferred_element_type=float32
    )
    grad_scores = probs_again * (
        grad_probs - jnp.sum(probs_again * grad_probs, axis=-1, keepdims=True)
    )
    grad_scores = grad_scores.astype(bfloat)
    grad_query = jnp.einsum(
        "nhqk,nkhd->nqhd", grad_scores, key_window, preferred_element_type=float32
    ) * HD ** (-0.5)
    grad_key_window = jnp.einsum(
        "nhqk,nqhd->nkhd", grad_scores, query_blocks, preferred_element_type=float32
    ) * HD ** (-0.5)
    grad_query = grad_query.reshape(token_rows, heads_local, HD)
    grad_keys = fold_window(grad_key_window, block)
    grad_values = fold_window(grad_value_window, block)
    grad_query_proj = query_pull(grad_query)[0]
    grad_key_proj = key_pull(grad_keys)[0]
    grad_value_proj = grad_values.reshape(token_rows, -1)
    grad_projected = jnp.stack([grad_query_proj, grad_key_proj, grad_value_proj], axis=1).astype(
        bfloat
    )
    both_branches = attn_branch + (mlp_half + mlp_came)
    out_mine = (layer_mine + both_branches).astype(bfloat)
    out_other = (layer_other + across(both_branches, 1)).astype(bfloat)
    layer_out = place_two(out_mine, out_other, core).reshape(token_rows, width)

    hidden_one_half = tensor_sum(
        lambda rows: jnp.einsum("tce,cde->td", rows, qkv_weight, preferred_element_type=float32),
        grad_projected,
    )
    grad_qkv = jnp.einsum(
        "td,tce->ced", hidden_one, grad_projected, preferred_element_type=float32
    )
    gain_grad_one = jnp.einsum("ced,cde->d", grad_qkv, qkv_weight.astype(float32)) / gain_one
    hidden_one_came = across(hidden_one_half, 2)
    late, gain_grad_one = dp_sum(
        [grad_qkv.reshape(3 * columns, width), grad_out], gain_grad_one, dp_size, 0
    )
    hidden_one_came, late = lax.optimization_barrier((hidden_one_came, late))
    grad_hidden_one = hidden_one_half + hidden_one_came
    norm_one_pull = jax.vjp(lambda rows: layer_norm(rows, gain_one), layer_mine)[1]
    both_norms = norm_two_part + norm_one_pull(grad_hidden_one)[0]
    input_mine = (cot_mine + both_norms).astype(bfloat)
    input_other = (cot_other + across(both_norms, 1)).astype(bfloat)
    input_grad = place_two(input_mine, input_other, core).reshape(token_rows, width)

    grad_qkv = late[: 3 * columns].reshape(3, columns, width)
    grad_out = late[3 * columns :]
    grad_qkv = grad_qkv.transpose(0, 2, 1)
    return (layer_out, input_grad, grad_qkv, grad_out, grad_up, grad_down, gain_grad_one, gain_grad_two)


def solution(mesh):
    return jax.shard_map(
        functools.partial(per_device, mesh.shape["tensor"], mesh.shape["dp"]),
        mesh=mesh,
        in_specs=(
            P("dp", None),
            P("dp"),
            P(None, None, "tensor"),
            P("tensor", None),
            P(None, None, "tensor"),
            P("tensor", None),
            P(),
            P(),
            P("dp", None),
        ),
        out_specs=(
            P("dp", None),
            P("dp", None),
            P(None, None, "tensor"),
            P("tensor", None),
            P(None, None, "tensor"),
            P("tensor", None),
            P(),
            P(),
        ),
        check_vma=False,
    )
```
